128 devices in a mesh: leaf: 64 (over z, y, x), sub: 2 (over core).
Axes of the slice: x: 4, y: 4, z: 4, core: 2. Of those that a mesh axis runs over, the one named last changes fastest.
Arguments:
- density: bfloat16 [8, 131072], P(None, ('leaf', 'sub')), may hold values from -6 to 6
- basis: bfloat16 [2048, 64, 64], P(('leaf', 'sub')), may hold values from -0.75 to 0.75
- near_ids: int32 [2048, 24], P(('leaf', 'sub')), may hold values from 0 to 159, as said below
- near_count: int32 [2048], P(('leaf', 'sub')), may hold values from 16 to 24
- near_blocks: bfloat16 [2048, 64, 1536], P(('leaf', 'sub')), may hold values from -0.15625 to 0.15625
- local_transfer: bfloat16 [1920, 64, 128], P(('leaf', 'sub')), may hold values from -0.5 to 0.5
- local_coupling: bfloat16 [3968, 64, 1024], P(('leaf', 'sub')), may hold values from -0.1875 to 0.1875
- local_coupling_ids: int32 [3968, 16], P(('leaf', 'sub')), may hold values from 0 to 159, as said below
- top_transfer: bfloat16 [126, 64, 128], replicated, may hold values from -0.5 to 0.5
- top_coupling: bfloat16 [126, 64, 128], replicated, may hold values from -0.5 to 0.5
- top_coupling_ids: int32 [126, 2], replicated, may hold values from 0 to 63, as said below
Outputs:
- potential: float32 [8, 131072], P(None, ('leaf', 'sub'))
The draws below stay inside these ranges and needn't reach their ends.
Inputs may be any that keep to these rules, and one draw needn't show every extreme that they name: `near_ids`: each entry is a window index of its leaf's device with n = 16; entries that name a device outside the slice read as zeros. `local_coupling_ids`: an entry of row r = d * 31 + 2 * 16 - 2 n + m is a window index of device d at the level of n = 16 >> h nodes a device, below 10 n. `top_coupling_ids`: an entry of row D - 2 n + m, for the level of n = D >> t nodes, names a node of that level, below n.
All inputs are finite; a program needn't handle non-finite values.
Results may differ from the reference program's by a relative error of at most 0.017.
Values may be sent and summed in bfloat16 or wider, within the bound.
No kernel may reach another device: no remote copies, remote signals or barrier semaphores. Data moves between devices by JAX's collectives and lax.ppermute only.
A program may use at most 64 MiB of HBM per device.

```python
import jax
import jax.numpy as jnp
from jax import lax

P_SIZE = 64
K = 64
NV = 8
LOCAL_LEVELS = 5
NEAR = 24
COUP = 16
COUP_TOP = 2
LEAF_DEV = 16
LOCAL_NODES = 31
LEAVES = 2048
POINTS = 131072
NODES = 3968
TRANSFERS = 1920
TOP_NODES = 126
N_LEAF = 64
N_SUB = 2


def window_ids(key, span_sizes, columns, highest):
    random_bits = jax.random.randint(key, (span_sizes.shape[0], columns), 0, 1 << 30, dtype=jnp.int32)
    chosen = random_bits % span_sizes[:, None]
    return chosen.at[0, 0].set(highest).at[0, 1].set(0).astype(jnp.int32)


def draw_near_ids(key, part):
    key = jax.random.fold_in(key, 1)
    span_sizes = jnp.full((LEAVES,), 10 * LEAF_DEV, dtype=jnp.int32)
    return window_ids(key, span_sizes, NEAR, 10 * LEAF_DEV - 1)


def draw_near_count(key, part):
    key = jax.random.fold_in(key, 2)
    lowest = NEAR - NEAR // 3
    counts = jax.random.randint(key, (LEAVES,), lowest, NEAR + 1, dtype=jnp.int32)
    return counts.at[0].set(NEAR).at[1].set(lowest)


def draw_local_coupling_ids(key, part):
    key = jax.random.fold_in(key, 3)
    within = jnp.arange(NODES, dtype=jnp.int32) % LOCAL_NODES
    span_sizes = jnp.zeros((NODES,), dtype=jnp.int32)
    for height in range(LOCAL_LEVELS):
        node_count = LEAF_DEV >> height
        offset = 2 * LEAF_DEV - 2 * node_count
        span_sizes = jnp.where(within >= offset, 10 * node_count, span_sizes)
    return window_ids(key, span_sizes, COUP, 10 * LEAF_DEV - 1)


def draw_top_coupling_ids(key, part):
    key = jax.random.fold_in(key, 4)
    devices = TOP_NODES + 2
    within = jnp.arange(TOP_NODES, dtype=jnp.int32)
    span_sizes = jnp.ones((TOP_NODES,), dtype=jnp.int32)
    for height in range(1, devices.bit_length() - 1):
        node_count = devices >> height
        offset = devices - 2 * node_count
        span_sizes = jnp.where(within >= offset, node_count, span_sizes)
    return window_ids(key, span_sizes, COUP_TOP, devices // 2 - 1)


def level_of(own_key, dims, shards, least, largest):
    loudness = 1.0
    for dim, shards_of in shards:
        heights = jax.random.uniform(jax.random.fold_in(jax.random.fold_in(own_key, 6), dim), (shards_of,), jnp.float32, least / len(shards), largest / len(shards))
        loudness = loudness * jnp.repeat(jnp.exp(heights), dims[dim] // shards_of).reshape((-1,) + (1,) * (len(dims) - 1 - dim))
    return loudness


def centred(stream_key, dims, scale, reach, split=(), held_as=jnp.bfloat16):
    values = scale * jax.random.normal(stream_key, dims, jnp.float32)
    if split:
        values = values * level_of(stream_key, dims, split, -0.22, 0.18)
    return jnp.clip(values, -reach, reach).astype(held_as)


def setup_inputs(seed: int = 0) -> dict:
    streams_of = jax.random.split(jax.random.key(seed), 12)
    density = centred(streams_of[0], (NV, POINTS), 1.0, 6.0, ((1, 128),))
    basis = centred(streams_of[1], (LEAVES, P_SIZE, K), P_SIZE ** -0.5, 0.75, ((0, 128),))
    near_ids = draw_near_ids(jax.random.fold_in(streams_of[11], 71), 0)
    near_count = draw_near_count(jax.random.fold_in(streams_of[11], 71), 0)
    near_blocks = centred(streams_of[4], (LEAVES, P_SIZE, NEAR * P_SIZE), (NEAR * P_SIZE) ** -0.5, 0.15625, ((0, 128),))
    local_transfer = centred(streams_of[5], (TRANSFERS, K, 2 * K), (2 * K) ** -0.5, 0.5, ((0, 128),))
    local_coupling = centred(streams_of[6], (NODES, K, COUP * K), (COUP * K) ** -0.5, 0.1875, ((0, 128),))
    local_coupling_ids = draw_local_coupling_ids(jax.random.fold_in(streams_of[11], 71), 0)
    top_transfer = centred(streams_of[8], (TOP_NODES, K, 2 * K), (2 * K) ** -0.5, 0.5)
    top_coupling = centred(streams_of[9], (TOP_NODES, K, COUP_TOP * K), (COUP_TOP * K) ** -0.5, 0.5)
    top_coupling_ids = draw_top_coupling_ids(jax.random.fold_in(streams_of[11], 71), 0)
    return {"density": density, "basis": basis, "near_ids": near_ids, "near_count": near_count, "near_blocks": near_blocks, "local_transfer": local_transfer, "local_coupling": local_coupling, "local_coupling_ids": local_coupling_ids, "top_transfer": top_transfer, "top_coupling": top_coupling, "top_coupling_ids": top_coupling_ids}


def rounded(values):
    return lax.optimization_barrier(values.astype(jnp.bfloat16)).astype(jnp.float32)


def blockwise(form, operand, blocks, groups):
    vectors, row_count, columns = operand.shape
    per_group = row_count // groups
    shaped = operand.reshape(vectors, groups, per_group, columns).transpose(1, 0, 2, 3)
    grouped = blocks.reshape((groups, per_group) + blocks.shape[1:])

    def block_apply(operands):
        return jnp.einsum(form, operands[0].astype(jnp.float32), operands[1].astype(jnp.float32))

    result = lax.map(block_apply, (shaped, grouped))
    return result.transpose(1, 0, 2, 3).reshape(vectors, row_count, -1)


def window_rows(values, slot_ids, per_device, live_mask):
    row_count = slot_ids.shape[0]
    devices = row_count // per_device
    device = jnp.arange(row_count, dtype=jnp.int32) // per_device
    source_dev = (2 * (device // 2) - 4)[:, None] + slot_ids // per_device
    source = source_dev * per_device + slot_ids % per_device
    inside = (source_dev >= 0) & (source_dev < devices) & live_mask
    picked = jnp.take(values, jnp.clip(source, 0, row_count - 1).astype(jnp.int32), axis=1)
    picked = jnp.where(inside[None, :, :, None], picked, jnp.zeros_like(picked))
    return picked.reshape(values.shape[0], row_count, -1)


def reference(density, basis, near_ids, near_count, near_blocks, local_transfer, local_coupling, local_coupling_ids, top_transfer, top_coupling, top_coupling_ids):
    devices = N_LEAF * N_SUB
    vectors = density.shape[0]
    leaf_count = basis.shape[0]
    shaped = density.reshape(vectors, leaf_count, P_SIZE)
    live_mask = jnp.arange(NEAR, dtype=jnp.int32)[None, :] < near_count[:, None]
    near_sources = window_rows(shaped, near_ids, LEAF_DEV, live_mask)
    near_field = blockwise('vnc,nkc->vnk', near_sources, near_blocks, devices)
    coeffs = [jnp.einsum('vlp,lpk->vlk', shaped.astype(jnp.float32), basis.astype(jnp.float32)).astype(jnp.bfloat16)]
    transfers = local_transfer.reshape(devices, LEAF_DEV - 1, K, 2 * K)
    for height in range(1, LOCAL_LEVELS):
        node_count = LEAF_DEV >> height
        offset = LEAF_DEV - 2 * node_count
        transfer = transfers[:, offset:offset + node_count].reshape(devices * node_count, K, 2 * K)
        children = coeffs[-1].reshape(vectors, devices * node_count, 2 * K)
        coeffs.append(blockwise('vnc,nkc->vnk', children, transfer, devices).astype(jnp.bfloat16))
    couplings = local_coupling.reshape(devices, LOCAL_NODES, K, COUP * K)
    coupling_ids = local_coupling_ids.reshape(devices, LOCAL_NODES, COUP)
    coupled = []
    for height in range(LOCAL_LEVELS):
        node_count = LEAF_DEV >> height
        offset = 2 * LEAF_DEV - 2 * node_count
        blocks = couplings[:, offset:offset + node_count].reshape(devices * node_count, K, COUP * K)
        slot_ids = coupling_ids[:, offset:offset + node_count].reshape(devices * node_count, COUP)
        operand = window_rows(coeffs[height], slot_ids, node_count, jnp.ones(slot_ids.shape, dtype=bool))
        coupled.append(blockwise('vnc,nkc->vnk', operand, blocks, devices))
    top_levels = devices.bit_length() - 1
    top_coeffs = [coeffs[-1]]
    top_coupled = [None]
    for height in range(1, top_levels):
        node_count = devices >> height
        offset = devices - 2 * node_count
        children = top_coeffs[-1].reshape(vectors, node_count, 2 * K).astype(jnp.float32)
        parent_coeffs = jnp.einsum('vnc,nkc->vnk', children, top_transfer[offset:offset + node_count].astype(jnp.float32)).astype(jnp.bfloat16)
        top_coeffs.append(parent_coeffs)
        picked = jnp.take(parent_coeffs, top_coupling_ids[offset:offset + node_count], axis=1)
        operand = picked.reshape(vectors, node_count, COUP_TOP * K).astype(jnp.float32)
        top_coupled.append(jnp.einsum('vnc,nkc->vnk', operand, top_coupling[offset:offset + node_count].astype(jnp.float32)))
    incoming = top_coupled[-1]
    for height in range(top_levels - 1, 0, -1):
        node_count = devices >> height
        offset = devices - 2 * node_count
        descent = jnp.einsum('vnk,nkc->vnc', rounded(incoming), top_transfer[offset:offset + node_count].astype(jnp.float32))
        descent = descent.reshape(vectors, 2 * node_count, K)
        incoming = top_coupled[height - 1] + descent if height > 1 else descent
    incoming = coupled[-1] + incoming
    for height in range(LOCAL_LEVELS - 1, 0, -1):
        node_count = LEAF_DEV >> height
        offset = LEAF_DEV - 2 * node_count
        transfer = transfers[:, offset:offset + node_count].reshape(devices * node_count, K, 2 * K)
        descent = blockwise('vnk,nkc->vnc', rounded(incoming), transfer, devices)
        incoming = coupled[height - 1] + descent.reshape(vectors, 2 * devices * node_count, K)
    far_field = jnp.einsum('vlk,lpk->vlp', rounded(incoming), basis.astype(jnp.float32))
    return (near_field + far_field).reshape(vectors, leaf_count * P_SIZE)
```

```python
import jax
import jax.numpy as jnp
from jax import lax
from jax.experimental import pallas as pl
from jax.experimental.pallas import tpu as pltpu
from jax.sharding import PartitionSpec as P

NV = 8
K = 64
LEAVES = 16
NEAR = 24
COUP = 16
HEIGHTS = 5
PAIRS = 24
NODES = 2 * PAIRS
LEVEL_OFFSETS = (16, 32, 40, 44, 46)
ZERO = 5 * 2 * NODES
TOP = 126
BF = jnp.bfloat16
F32 = jnp.float32


def dot(a, b):
    return lax.dot_general(a, b, (((1,), (0,)), ((), ())), preferred_element_type=F32)


def dot_t(a, b):
    return lax.dot_general(a, b, (((1,), (1,)), ((), ())), preferred_element_type=F32)


def beside(a, b):
    return jnp.concatenate([a, b], axis=1)


def window_nodes(ids, height, offset, leaf, sub, live):
    shift = 4 - height
    slot = jnp.right_shift(ids, shift)
    node = jnp.bitwise_and(ids, (1 << shift) - 1)
    delta = jnp.right_shift(slot, 1) - 2
    core = jnp.bitwise_and(slot, 1)
    chip = leaf + delta
    near_flip = jnp.bitwise_and(leaf, 1) ^ sub
    far_flip = jnp.bitwise_and(jnp.right_shift(leaf, 1), 1) ^ sub
    place = jnp.where(delta == 1, 1 + near_flip, jnp.where(delta == -1, 2 - near_flip, 0))
    place = jnp.where(delta == 2, 3 + far_flip, jnp.where(delta == -2, 4 - far_flip, place))
    index = (place * 2 + core) * NODES + offset + node
    live = live & (chip >= 0) & (chip < 64)
    index = jnp.where(live, index, ZERO)
    column = lax.broadcasted_iota(jnp.int32, ids.shape, 1)
    return index ^ jnp.bitwise_and(column, 1)


def upward_kernel(
    density, basis, transfer, near_ids, near_count, coupling_ids, pack, roots, near_nodes, coupling_nodes
):
    leaf, sub = lax.axis_index("leaf"), lax.axis_index("sub")
    level = []
    for p in range(8):
        pair = density[:, 128 * p : 128 * p + 128]
        pack[p] = pair
        joined = beside(dot(pair[:, :K], basis[2 * p]), dot(pair[:, K:], basis[2 * p + 1])).astype(BF)
        pack[8 + p] = joined
        level.append(joined)
    row, first = 16, 0
    while len(level) > 1:
        nodes = [dot_t(pair, transfer[first + m]) for m, pair in enumerate(level)]
        first += len(level)
        level = [beside(nodes[q], nodes[q + 1]).astype(BF) for q in range(0, len(nodes), 2)]
        for pair in level:
            pack[row] = pair
            row += 1
    root = dot_t(level[0], transfer[first])
    pack[row] = beside(root, root).astype(BF)
    sent = beside(root[:4], root[4:]).astype(BF)
    roots[...] = jnp.broadcast_to(sent[None], roots.shape)
    slots = lax.broadcasted_iota(jnp.int32, near_ids.shape, 1)
    near_nodes[...] = window_nodes(near_ids[...], 0, 0, leaf, sub, slots < near_count[...])
    for height in range(HEIGHTS):
        count = LEAVES >> height
        at = 2 * LEAVES - 2 * count
        ids = coupling_ids[at : at + count]
        coupling_nodes[at : at + count] = window_nodes(
            ids, height, LEVEL_OFFSETS[height], leaf, sub, ids >= 0
        )


def window_kernel(
    own, near_mine, near_other, far_mine, far_other, near_nodes, coupling_nodes, near_blocks, coupling,
    transfer, basis, partial, onward, window, near_held, coupling_held, near_sems, coupling_sems,
):
    near_copies = [
        pltpu.make_async_copy(near_blocks.at[pl.ds(4 * i, 4)], near_held.at[pl.ds(4 * i, 4)], near_sems.at[i])
        for i in range(4)
    ]
    spans = [(0, 4), (4, 4), (8, 4), (12, 4), (16, 8), (24, 7)]
    coupling_copies = [
        pltpu.make_async_copy(coupling.at[pl.ds(a, n)], coupling_held.at[pl.ds(a, n)], coupling_sems.at[i])
        for i, (a, n) in enumerate(spans)
    ]
    for copy in near_copies + coupling_copies:
        copy.start()
    for place, arrived in enumerate((own, near_mine, near_other, far_mine, far_other)):
        for p in range(2 * PAIRS):
            pair = arrived[p].astype(F32)
            at = 2 * (place * 2 * PAIRS + p)
            window[at] = pair
            window[at + 1] = pltpu.roll(pair, K, 1)
    window[ZERO] = jnp.zeros((NV, 128), F32)
    window[ZERO + 1] = jnp.zeros((NV, 128), F32)
    low = lax.broadcasted_iota(jnp.int32, (NV, 128), 1) < K

    def gathered(nodes, row, slots):
        parts = [
            jnp.where(low, window[nodes[row, j]], window[nodes[row, j + 1]]) for j in range(0, slots, 2)
        ]
        return jnp.concatenate(parts, axis=1).astype(BF)

    near = []
    for i in range(LEAVES):
        if i % 4 == 0:
            near_copies[i // 4].wait()
        near.append(dot_t(gathered(near_nodes, i, NEAR), near_held[i]))
    for i in range(0, LEAVES, 2):
        partial[:, K * i : K * i + 128] = beside(near[i], near[i + 1])
    coupled = []
    starts = {a: i for i, (a, _) in enumerate(spans)}
    for r in range(2 * LEAVES - 1):
        if r in starts:
            coupling_copies[starts[r]].wait()
        coupled.append(dot_t(gathered(coupling_nodes, r, COUP), coupling_held[r]))
    eye = (
        lax.broadcasted_iota(jnp.int32, (K, K), 0) == lax.broadcasted_iota(jnp.int32, (K, K), 1)
    ).astype(F32)
    state = [jnp.concatenate([coupled[30], eye], axis=0)]
    for height in range(HEIGHTS - 1, 0, -1):
        count = LEAVES >> height
        at, offset = 2 * LEAVES - 4 * count, LEAVES - 2 * count
        below = []
        for m in range(count):
            descent = dot(state[m].astype(BF), transfer[offset + m])
            added = beside(coupled[at + 2 * m], coupled[at + 2 * m + 1])
            top = descent[:NV] + added
            rest = descent[NV:]
            for half in (slice(0, K), slice(K, 128)):
                below.append(jnp.concatenate([top[:, half], rest[:, half]], axis=0))
        state = below
    for i in range(0, LEAVES, 2):
        pair = beside(dot_t(state[i].astype(BF), basis[i]), dot_t(state[i + 1].astype(BF), basis[i + 1]))
        span = slice(K * i, K * i + 128)
        partial[:, span] = partial[:, span] + pair[:NV]
        onward[:, span] = pair[NV:].astype(BF)


def top_kernel(
    roots, transfer, coupling, ids, partial, onward, potential, nodes, held, sems
):
    device = lax.axis_index("leaf") * 2 + lax.axis_index("sub")
    firsts = [128 - (128 >> (t - 1)) for t in range(1, 7)]
    rows = [first + jnp.right_shift(device, t) for t, first in enumerate(firsts, 1)]
    copies = [pltpu.make_async_copy(coupling.at[row], held.at[t], sems.at[t]) for t, row in enumerate(rows)]
    for copy in copies:
        copy.start()
    low4 = lax.broadcasted_iota(jnp.int32, (4, 128), 1) < K
    level = []
    for m in range(64):
        a, b = roots[2 * m].astype(F32), roots[2 * m + 1].astype(F32)
        upper = jnp.where(low4, a, pltpu.roll(b, K, 1))
        lower = jnp.where(low4, pltpu.roll(a, K, 1), b)
        level.append(jnp.concatenate([upper, lower], axis=0))
    for first in firsts:
        made = [dot_t(pair.astype(BF), transfer[first + m]) for m, pair in enumerate(level)]
        level = []
        for m in range(0, len(made), 2):
            pair = beside(made[m], made[m + 1]).astype(BF).astype(F32)
            nodes[first + m] = pair
            nodes[first + m + 1] = pltpu.roll(pair, K, 1)
            level.append(pair)
    low = lax.broadcasted_iota(jnp.int32, (NV, 128), 1) < K
    incoming = None
    for t in range(6, 0, -1):
        row = rows[t - 1]
        copies[t - 1].wait()
        first = firsts[t - 1]
        operand = jnp.where(low, nodes[first + ids[row, 0]], nodes[first + (ids[row, 1] ^ 1)])
        coupled = dot_t(operand.astype(BF), held[t - 1])
        incoming = coupled if incoming is None else incoming + coupled
        descent = dot(incoming.astype(BF), transfer[row])
        right = jnp.bitwise_and(jnp.right_shift(device, t - 1), 1) == 1
        incoming = jnp.where(right, descent[:, K:], descent[:, :K])
    potential[...] = partial[...] + dot(incoming.astype(BF), onward[...])


def spec(space):
    return pl.BlockSpec(memory_space=space)


VMEM, SMEM, ANY = pltpu.VMEM, pltpu.SMEM, pl.ANY


def swapped(first, second):
    return [(2 * c, 2 * (first(c) % 64)) for c in range(64)] + [
        (2 * c + 1, 2 * (second(c) % 64) + 1) for c in range(64)
    ]


NEXT = swapped(lambda c: c ^ 1, lambda c: ((c + 1) ^ 1) - 1)
SECOND = swapped(lambda c: c ^ 2, lambda c: ((c + 2) ^ 2) - 2)


def local(
    density, basis, near_ids, near_count, near_blocks, local_transfer, local_coupling, local_coupling_ids,
    top_transfer, top_coupling, top_coupling_ids,
):
    shape = jax.ShapeDtypeStruct
    pack, roots, near_nodes, coupling_nodes = pl.pallas_call(
        upward_kernel,
        out_shape=(
            shape((PAIRS, NV, 128), BF),
            shape((128, 4, 128), BF),
            shape((LEAVES, NEAR), jnp.int32),
            shape((2 * LEAVES - 1, COUP), jnp.int32),
        ),
        in_specs=[spec(VMEM)] * 6,
        out_specs=(spec(VMEM),) * 4,
        name="upward",
    )(density, basis, local_transfer, near_ids, near_count.reshape(LEAVES, 1), local_coupling_ids)
    every = ("leaf", "sub")
    own = lax.all_gather(pack, "sub", axis=0, tiled=True)
    near_mine = lax.ppermute(own, every, NEXT)
    far_mine = lax.ppermute(own, every, SECOND)
    all_roots = lax.all_to_all(roots, every, 0, 0, tiled=True)
    near_other = lax.ppermute(near_mine, "sub", [(0, 1), (1, 0)])
    far_other = lax.ppermute(far_mine, "sub", [(0, 1), (1, 0)])
    partial, onward = pl.pallas_call(
        window_kernel,
        out_shape=(shape((NV, 1024), F32), shape((K, 1024), BF)),
        in_specs=[spec(VMEM)] * 5 + [spec(SMEM)] * 2 + [spec(ANY)] * 2 + [spec(VMEM)] * 2,
        out_specs=(spec(VMEM),) * 2,
        scratch_shapes=[
            pltpu.VMEM((ZERO + 2, NV, 128), F32),
            pltpu.VMEM((LEAVES, 64, NEAR * 64), BF),
            pltpu.VMEM((2 * LEAVES - 1, K, COUP * K), BF),
            pltpu.SemaphoreType.DMA((4,)),
            pltpu.SemaphoreType.DMA((6,)),
        ],
        compiler_params=pltpu.CompilerParams(vmem_limit_bytes=24 << 20),
        cost_estimate=pl.CostEstimate(flops=120_000_000, bytes_accessed=8_000_000, transcendentals=0),
        name="window",
    )(
        own, near_mine, near_other, far_mine, far_other, near_nodes, coupling_nodes, near_blocks,
        local_coupling, local_transfer, basis,
    )
    return pl.pallas_call(
        top_kernel,
        out_shape=shape((NV, 1024), F32),
        in_specs=[spec(VMEM), spec(VMEM), spec(ANY), spec(SMEM), spec(VMEM), spec(VMEM)],
        out_specs=spec(VMEM),
        scratch_shapes=[
            pltpu.VMEM((TOP, NV, 128), F32),
            pltpu.VMEM((6, K, 128), BF),
            pltpu.SemaphoreType.DMA((6,)),
        ],
        compiler_params=pltpu.CompilerParams(vmem_limit_bytes=16 << 20),
        name="top",
    )(all_roots, top_transfer, top_coupling, top_coupling_ids, partial, onward)


def solution(mesh):
    in_specs = (
        P(None, ("leaf", "sub")),
        P(("leaf", "sub"), None, None),
        P(("leaf", "sub"), None),
        P(("leaf", "sub")),
        P(("leaf", "sub"), None, None),
        P(("leaf", "sub"), None, None),
        P(("leaf", "sub"), None, None),
        P(("leaf", "sub"), None),
        P(),
        P(),
        P(),
    )
    out_specs = P(None, ("leaf", "sub"))
    return jax.shard_map(local, mesh=mesh, in_specs=in_specs, out_specs=out_specs, check_vma=False)
```

```python
import jax
import jax.numpy as jnp
from jax import lax
from jax.experimental import pallas as pl
from jax.experimental.pallas import tpu as pltpu
from jax.sharding import PartitionSpec as P

NV = 8
K = 64
LEAVES = 16
NEAR = 24
COUP = 16
HEIGHTS = 5
PAIRS = 24
NODES = 2 * PAIRS
LEVEL_OFFSETS = (16, 32, 40, 44, 46)
ZERO = 5 * 2 * NODES
TOP = 126
AHEAD = 3
FIRSTS = (0, 64, 96, 112, 120, 124)
BF = jnp.bfloat16
F32 = jnp.float32


def dot(a, b):
    return lax.dot_general(a, b, (((1,), (0,)), ((), ())), preferred_element_type=F32)


def dot_t(a, b):
    return lax.dot_general(a, b, (((1,), (1,)), ((), ())), preferred_element_type=F32)


def unit(n):
    return (lax.broadcasted_iota(jnp.int32, (n, n), 0) == lax.broadcasted_iota(jnp.int32, (n, n), 1)).astype(BF)


def stacked(*parts):
    return jnp.concatenate(parts, axis=0)


def turned(columns):
    high = columns.astype(BF)
    rest = (columns - high.astype(F32)).astype(BF)
    return dot_t(unit(NV), high) + dot_t(unit(NV), rest)


def beside(a, b):
    return jnp.concatenate([a, b], axis=1)


def window_nodes(ids, height, offset, leaf, sub, live, slot_axis):
    shift = jnp.broadcast_to(4 - height, ids.shape)
    slot = jnp.right_shift(ids, shift)
    node = ids - jnp.left_shift(slot, shift)
    delta = jnp.right_shift(slot, 1) - 2
    core = jnp.bitwise_and(slot, 1)
    chip = leaf + delta
    near_flip = jnp.bitwise_and(leaf, 1) ^ sub
    far_flip = jnp.bitwise_and(jnp.right_shift(leaf, 1), 1) ^ sub
    place = jnp.where(delta == 1, 1 + near_flip, jnp.where(delta == -1, 2 - near_flip, 0))
    place = jnp.where(delta == 2, 3 + far_flip, jnp.where(delta == -2, 4 - far_flip, place))
    index = (place * 2 + core) * NODES + offset + node
    live = live & (chip >= 0) & (chip < 64)
    index = jnp.where(live, index, ZERO)
    column = lax.broadcasted_iota(jnp.int32, ids.shape, slot_axis)
    return index ^ jnp.bitwise_and(column, 1)


def upward_kernel(
    density, basis, transfer, near_ids, near_count, coupling_ids, pack, roots, near_nodes, coupling_nodes
):
    leaf, sub = lax.axis_index("leaf"), lax.axis_index("sub")
    level = []
    for p in range(8):
        pair = density[:, 128 * p : 128 * p + 128]
        pack[p] = pair
        joined = beside(dot(pair[:, :K], basis[2 * p]), dot(pair[:, K:], basis[2 * p + 1])).astype(BF)
        pack[8 + p] = joined
        level.append(joined)
    made = [dot_t(transfer[m], pair).astype(BF) for m, pair in enumerate(level)]
    columns, first = list(made), 8
    while len(made) > 1:
        made = [
            dot(transfer[first + q], stacked(made[2 * q], made[2 * q + 1])).astype(BF)
            for q in range(len(made) // 2)
        ]
        first += len(made)
        columns += made
    rows = dot_t(unit(NV), stacked(*columns))
    for q in range(7):
        pack[16 + q] = rows[:, 128 * q : 128 * q + 128].astype(BF)
    root = rows[:, 896:]
    pack[23] = beside(root, root).astype(BF)
    sent = beside(root[:4], root[4:]).astype(BF)
    roots[...] = jnp.broadcast_to(sent[None], roots.shape)
    slots = lax.broadcasted_iota(jnp.int32, near_ids.shape, 1)
    diagonal = lax.broadcasted_iota(jnp.int32, (LEAVES, LEAVES), 0) == lax.broadcasted_iota(
        jnp.int32, (LEAVES, LEAVES), 1
    )
    counts = jnp.sum(jnp.where(diagonal, near_count[...], 0), axis=1, keepdims=True)
    near_nodes[...] = window_nodes(near_ids[...], 0, 0, leaf, sub, slots < counts, 1)
    ids = coupling_ids[...]
    rows = lax.broadcasted_iota(jnp.int32, ids.shape, 1)
    height = sum((rows >= 2 * LEAVES - 2 * (LEAVES >> h)).astype(jnp.int32) for h in range(1, HEIGHTS))
    offset = jnp.zeros(ids.shape, jnp.int32)
    for h, place in enumerate(LEVEL_OFFSETS):
        offset = jnp.where(height == h, place, offset)
    coupling_nodes[...] = window_nodes(ids, height, offset, leaf, sub, ids >= 0, 0)


def window_kernel(
    own, near_mine, near_other, far_mine, far_other, near_nodes, coupling_nodes, near_blocks, coupling,
    transfer, basis, top_transfer, top_coupling, partial, onward, shares, window, arrived, near_ids,
    coupling_ids, near_held, coupling_held, transfer_held, basis_held, rows_held, links_held, id_sems,
    arrival_sems, near_sems, coupling_sems, small_sems, row_sems, link_sems,
):
    device = lax.axis_index("leaf") * 2 + lax.axis_index("sub")
    copy = pltpu.make_async_copy
    id_copies = [copy(coupling_nodes, coupling_ids, id_sems.at[0]), copy(near_nodes, near_ids, id_sems.at[1])]
    arrivals = [
        copy(source, arrived.at[i], arrival_sems.at[i])
        for i, source in enumerate((own, near_mine, near_other, far_mine, far_other))
    ]
    small_copies = [copy(transfer, transfer_held, small_sems.at[0]), copy(basis, basis_held, small_sems.at[1])]
    places = [first + jnp.right_shift(device, t) for t, first in enumerate(FIRSTS, 1)]
    row_copies = [copy(top_transfer.at[row], rows_held.at[t], row_sems.at[t]) for t, row in enumerate(places)]
    link_copies = [copy(top_coupling.at[row], links_held.at[t], link_sems.at[t]) for t, row in enumerate(places)]
    coupling_copies = [
        copy(coupling.at[pl.ds(a, n)], coupling_held.at[pl.ds(a, n)], coupling_sems.at[i])
        for i, (a, n) in enumerate(((16, 15), (0, 16)))
    ]
    near_copies = [
        copy(near_blocks.at[pl.ds(a, 8)], near_held.at[pl.ds(a, 8)], near_sems.at[a // 8])
        for a in range(0, LEAVES, 8)
    ]
    queue = coupling_copies + near_copies
    for one in id_copies + arrivals + queue[:1] + row_copies + link_copies + small_copies + queue[1:AHEAD]:
        one.start()

    def take(index):
        queue[index].wait()
        if index + AHEAD < len(queue):
            queue[index + AHEAD].start()

    window[ZERO] = jnp.zeros((NV, 128), F32)
    window[ZERO + 1] = jnp.zeros((NV, 128), F32)
    for one in arrivals:
        one.wait()
    for place in range(5):
        for p in range(2 * PAIRS):
            pair = arrived[place, p].astype(F32)
            at = 2 * (place * 2 * PAIRS + p)
            window[at] = pair
            window[at + 1] = pltpu.roll(pair, K, 1)
    low = lax.broadcasted_iota(jnp.int32, (NV, 128), 1) < K

    def gathered(node, slots):
        parts = [jnp.where(low, window[node(j)], window[node(j + 1)]) for j in range(0, slots, 2)]
        return jnp.concatenate(parts, axis=1).astype(BF)

    def coupled(r):
        return dot_t(gathered(lambda j: coupling_ids[j, r], COUP), coupling_held[r])

    def near(i):
        return dot_t(gathered(lambda j: near_ids[i, j], NEAR), near_held[i])

    def descend(node, transfer_row, first):
        return dot(node.astype(BF), transfer_held[transfer_row]), beside(coupled_rows[first], coupled_rows[first + 1])

    def split(descent, added):
        top, rest = descent[:NV] + added, descent[NV:]
        return [stacked(top[:, :K], rest[:, :K]), stacked(top[:, K:], rest[:, K:])]

    def level(state, height):
        count = LEAVES >> height
        at, offset = 2 * LEAVES - 4 * count, LEAVES - 2 * count
        made = [descend(state[m], offset + m, at + 2 * m) for m in range(count)]
        return [child for one in made for child in split(*one)]

    for one in id_copies + row_copies + link_copies + small_copies:
        one.wait()
    coupled_rows = {}
    path = unit(K)
    take(0)
    for t in range(6):
        right = jnp.bitwise_and(jnp.right_shift(device, t), 1) == 1
        step = jnp.where(right, rows_held[t, :, K:], rows_held[t, :, :K])
        path = dot_t(path, step).astype(BF)
        for r in range(30 - 3 * t, max(27 - 3 * t, 15), -1):
            coupled_rows[r] = coupled(r)
        shares[:, 128 * t : 128 * t + 128] = dot(path, links_held[t]).astype(BF)
    state = [stacked(coupled_rows[30], unit(K).astype(F32))]
    take(1)
    for height in (4, 3, 2):
        state = level(state, height)
        for r in range(5 * (4 - height), 5 * (4 - height) + 5):
            coupled_rows[r] = coupled(r)
    coupled_rows[15] = coupled(15)
    take(2)
    near_rows = [near(i) for i in range(2)]
    state = level(state, 1)
    near_rows += [near(i) for i in range(2, 8)]
    ends = [dot_t(state[i].astype(BF), basis_held[i]) for i in range(LEAVES)]
    take(3)
    near_rows += [near(i) for i in range(8, LEAVES)]
    for i in range(0, LEAVES, 2):
        span = slice(K * i, K * i + 128)
        pair = beside(ends[i], ends[i + 1])
        partial[:, span] = pair[:NV] + beside(near_rows[i], near_rows[i + 1])
        onward[:, span] = pair[NV:].astype(BF)


def top_kernel(
    roots, transfer, ids, partial, onward, shares, potential, nodes, held_ids, held, roots_held, partial_held,
    onward_held, shares_held, sems,
):
    device = lax.axis_index("leaf") * 2 + lax.axis_index("sub")
    copy = pltpu.make_async_copy
    root_copy = copy(roots, roots_held, sems.at[0])
    spans = ((0, 32), (32, 32), (64, 62))
    copies = [
        copy(transfer.at[pl.ds(a, n)], held.at[pl.ds(a, n)], sems.at[1 + i]) for i, (a, n) in enumerate(spans)
    ]
    id_copy = copy(ids, held_ids, sems.at[4])
    last_copies = [
        copy(shares, shares_held, sems.at[5]),
        copy(onward, onward_held, sems.at[6]),
        copy(partial, partial_held, sems.at[7]),
    ]
    for one in [root_copy] + copies + [id_copy] + last_copies:
        one.start()
    low4 = lax.broadcasted_iota(jnp.int32, (4, 128), 1) < K
    root_copy.wait()
    made = []
    for m in range(64):
        a, b = roots_held[2 * m].astype(F32), roots_held[2 * m + 1].astype(F32)
        upper = jnp.where(low4, a, pltpu.roll(b, K, 1))
        lower = jnp.where(low4, pltpu.roll(a, K, 1), b)
        if m % 32 == 0:
            copies[m // 32].wait()
        made.append(dot_t(held[m], stacked(upper, lower).astype(BF)).astype(BF))
    copies[2].wait()
    for t, first in enumerate(FIRSTS):
        if t:
            made = [
                dot(held[first + m], stacked(made[2 * m], made[2 * m + 1])).astype(BF)
                for m in range(len(made) // 2)
            ]
        for m, node in enumerate(made):
            nodes[first + m] = node
    id_copy.wait()
    sources = []
    for t, first in enumerate(FIRSTS, 1):
        row = first + jnp.right_shift(device, t)
        sources += [nodes[first + held_ids[0, row]], nodes[first + held_ids[1, row]]]
    for one in last_copies:
        one.wait()
    incoming = dot(shares_held[...], stacked(*sources)).astype(BF)
    incoming = dot_t(unit(NV), incoming).astype(BF)
    potential[...] = partial_held[...] + dot(incoming, onward_held[...])


def spec(space):
    return pl.BlockSpec(memory_space=space)


VMEM, SMEM, ANY = pltpu.VMEM, pltpu.SMEM, pl.ANY


def swapped(first, second):
    return [(2 * c, 2 * (first(c) % 64)) for c in range(64)] + [
        (2 * c + 1, 2 * (second(c) % 64) + 1) for c in range(64)
    ]


NEXT = swapped(lambda c: c ^ 1, lambda c: ((c + 1) ^ 1) - 1)
SECOND = swapped(lambda c: c ^ 2, lambda c: ((c + 2) ^ 2) - 2)


def local(
    density, basis, near_ids, near_count, near_blocks, local_transfer, local_coupling, local_coupling_ids,
    top_transfer, top_coupling, top_coupling_ids,
):
    shape = jax.ShapeDtypeStruct
    pack, roots, near_nodes, coupling_nodes = pl.pallas_call(
        upward_kernel,
        out_shape=(
            shape((PAIRS, NV, 128), BF),
            shape((128, 4, 128), BF),
            shape((LEAVES, NEAR), jnp.int32),
            shape((COUP, 2 * LEAVES - 1), jnp.int32),
        ),
        in_specs=[spec(VMEM)] * 6,
        out_specs=(spec(VMEM),) * 4,
        cost_estimate=pl.CostEstimate(flops=20_000_000, bytes_accessed=1_000_000, transcendentals=0),
        compiler_params=pltpu.CompilerParams(vmem_limit_bytes=56 << 20),
        name="upward",
    )(density, basis, local_transfer, near_ids, near_count.reshape(1, LEAVES), local_coupling_ids.T)
    every = ("leaf", "sub")
    own = lax.all_gather(pack, "sub", axis=0, tiled=True)
    near_mine = lax.ppermute(own, every, NEXT)
    far_mine = lax.ppermute(own, every, SECOND)
    all_roots = lax.all_to_all(roots, every, 0, 0, tiled=True)
    near_other = lax.ppermute(near_mine, "sub", [(0, 1), (1, 0)])
    far_other = lax.ppermute(far_mine, "sub", [(0, 1), (1, 0)])
    partial, onward, shares = pl.pallas_call(
        window_kernel,
        out_shape=(
            shape((NV, 1024), F32),
            shape((K, 1024), BF),
            shape((K, 768), BF),
        ),
        in_specs=[spec(ANY)] * 13,
        out_specs=(spec(VMEM),) * 3,
        scratch_shapes=[
            pltpu.VMEM((ZERO + 2, NV, 128), F32),
            pltpu.VMEM((5, 2 * PAIRS, NV, 128), BF),
            pltpu.SMEM((LEAVES, NEAR), jnp.int32),
            pltpu.SMEM((COUP, 2 * LEAVES - 1), jnp.int32),
            pltpu.VMEM((LEAVES, 64, NEAR * 64), BF),
            pltpu.VMEM((2 * LEAVES - 1, K, COUP * K), BF),
            pltpu.VMEM((LEAVES - 1, K, 128), BF),
            pltpu.VMEM((LEAVES, 64, K), BF),
            pltpu.VMEM((6, K, 128), BF),
            pltpu.VMEM((6, K, 128), BF),
            pltpu.SemaphoreType.DMA((2,)),
            pltpu.SemaphoreType.DMA((5,)),
            pltpu.SemaphoreType.DMA((4,)),
            pltpu.SemaphoreType.DMA((3,)),
            pltpu.SemaphoreType.DMA((2,)),
            pltpu.SemaphoreType.DMA((6,)),
            pltpu.SemaphoreType.DMA((6,)),
        ],
        compiler_params=pltpu.CompilerParams(vmem_limit_bytes=56 << 20),
        cost_estimate=pl.CostEstimate(flops=120_000_000, bytes_accessed=8_000_000, transcendentals=0),
        name="window",
    )(
        own, near_mine, near_other, far_mine, far_other, near_nodes, coupling_nodes, near_blocks,
        local_coupling, local_transfer, basis, top_transfer, top_coupling,
    )
    return pl.pallas_call(
        top_kernel,
        out_shape=shape((NV, 1024), F32),
        in_specs=[spec(ANY)] * 6,
        out_specs=spec(VMEM),
        scratch_shapes=[
            pltpu.VMEM((TOP, K, NV), BF),
            pltpu.SMEM((2, TOP), jnp.int32),
            pltpu.VMEM((TOP, K, 128), BF),
            pltpu.VMEM((128, 4, 128), BF),
            pltpu.VMEM((NV, 1024), F32),
            pltpu.VMEM((K, 1024), BF),
            pltpu.VMEM((K, 768), BF),
            pltpu.SemaphoreType.DMA((8,)),
        ],
        compiler_params=pltpu.CompilerParams(vmem_limit_bytes=56 << 20),
        name="top",
    )(all_roots, top_transfer, top_coupling_ids.T, partial, onward, shares)


def solution(mesh):
    in_specs = (
        P(None, ("leaf", "sub")),
        P(("leaf", "sub"), None, None),
        P(("leaf", "sub"), None),
        P(("leaf", "sub")),
        P(("leaf", "sub"), None, None),
        P(("leaf", "sub"), None, None),
        P(("leaf", "sub"), None, None),
        P(("leaf", "sub"), None),
        P(),
        P(),
        P(),
    )
    out_specs = P(None, ("leaf", "sub"))
    return jax.shard_map(local, mesh=mesh, in_specs=in_specs, out_specs=out_specs, check_vma=False)
```

```python
import jax
import jax.numpy as jnp
from jax import lax
from jax.experimental import pallas as pl
from jax.experimental.pallas import tpu as pltpu
from jax.sharding import PartitionSpec as P

NV = 8
K = 64
LEAVES = 16
NEAR = 24
COUP = 16
HEIGHTS = 5
PAIRS = 24
NODES = 2 * PAIRS
LEVEL_OFFSETS = (16, 32, 40, 44, 46)
ZERO = 5 * 2 * NODES
TOP = 126
AHEAD = 3
FIRSTS = (0, 64, 96, 112, 120, 124)
BF = jnp.bfloat16
F32 = jnp.float32


def dot(a, b):
    return lax.dot_general(a, b, (((1,), (0,)), ((), ())), preferred_element_type=F32)


def dot_t(a, b):
    return lax.dot_general(a, b, (((1,), (1,)), ((), ())), preferred_element_type=F32)


def unit(n):
    return (lax.broadcasted_iota(jnp.int32, (n, n), 0) == lax.broadcasted_iota(jnp.int32, (n, n), 1)).astype(BF)


def stacked(*parts):
    return jnp.concatenate(parts, axis=0)


def turned(columns):
    high = columns.astype(BF)
    rest = (columns - high.astype(F32)).astype(BF)
    return dot_t(unit(NV), high) + dot_t(unit(NV), rest)


def beside(a, b):
    return jnp.concatenate([a, b], axis=1)


def window_nodes(ids, height, offset, leaf, sub, live, slot_axis):
    shift = jnp.broadcast_to(4 - height, ids.shape)
    slot = jnp.right_shift(ids, shift)
    node = ids - jnp.left_shift(slot, shift)
    delta = jnp.right_shift(slot, 1) - 2
    core = jnp.bitwise_and(slot, 1)
    chip = leaf + delta
    near_flip = jnp.bitwise_and(leaf, 1) ^ sub
    far_flip = jnp.bitwise_and(jnp.right_shift(leaf, 1), 1) ^ sub
    place = jnp.where(delta == 1, 1 + near_flip, jnp.where(delta == -1, 2 - near_flip, 0))
    place = jnp.where(delta == 2, 3 + far_flip, jnp.where(delta == -2, 4 - far_flip, place))
    end_next = ((leaf == 0) | (leaf == 62)) & (delta == 1)
    end_last = ((leaf == 1) | (leaf == 63)) & (delta == -1)
    place = jnp.where(end_next | end_last, 4 - sub, place)
    index = (place * 2 + core) * NODES + offset + node
    live = live & (chip >= 0) & (chip < 64)
    index = jnp.where(live, index, ZERO)
    column = lax.broadcasted_iota(jnp.int32, ids.shape, slot_axis)
    return index ^ jnp.bitwise_and(column, 1)


def all_window_nodes(near_ids, near_count, coupling_ids):
    leaf, sub = lax.axis_index("leaf"), lax.axis_index("sub")
    slots = lax.broadcasted_iota(jnp.int32, near_ids.shape, 1)
    diagonal = lax.broadcasted_iota(jnp.int32, (LEAVES, LEAVES), 0) == lax.broadcasted_iota(
        jnp.int32, (LEAVES, LEAVES), 1
    )
    counts = jnp.sum(jnp.where(diagonal, near_count, 0), axis=1, keepdims=True)
    near_nodes = window_nodes(near_ids, 0, 0, leaf, sub, slots < counts, 1)
    rows = lax.broadcasted_iota(jnp.int32, coupling_ids.shape, 1)
    height = sum((rows >= 2 * LEAVES - 2 * (LEAVES >> h)).astype(jnp.int32) for h in range(1, HEIGHTS))
    offset = jnp.zeros(coupling_ids.shape, jnp.int32)
    for h, place in enumerate(LEVEL_OFFSETS):
        offset = jnp.where(height == h, place, offset)
    coupling_nodes = window_nodes(coupling_ids, height, offset, leaf, sub, coupling_ids >= 0, 0)
    return near_nodes, coupling_nodes


def upward_kernel(density, basis, transfer, pack, roots):
    level = []
    for p in range(8):
        pair = density[:, 128 * p : 128 * p + 128]
        pack[p] = pair
        joined = beside(dot(pair[:, :K], basis[2 * p]), dot(pair[:, K:], basis[2 * p + 1])).astype(BF)
        pack[8 + p] = joined
        level.append(joined)
    made = [dot_t(transfer[m], pair).astype(BF) for m, pair in enumerate(level)]
    columns, first = list(made), 8
    while len(made) > 1:
        made = [
            dot(transfer[first + q], stacked(made[2 * q], made[2 * q + 1])).astype(BF)
            for q in range(len(made) // 2)
        ]
        first += len(made)
        columns += made
    rows = dot_t(unit(NV), stacked(*columns))
    for q in range(7):
        pack[16 + q] = rows[:, 128 * q : 128 * q + 128].astype(BF)
    root = rows[:, 896:]
    pack[23] = beside(root, root).astype(BF)
    sent = beside(root[:4], root[4:]).astype(BF)
    roots[...] = jnp.broadcast_to(sent[None], roots.shape)


def window_kernel(
    own, near_mine, near_other, far_mine, far_other, near_ids_in, near_count_in, coupling_ids_in, near_blocks,
    coupling, transfer, basis, top_transfer, top_coupling, partial, onward, shares, window, arrived, near_raw,
    near_count, coupling_raw, near_nodes, coupling_nodes, near_ids, coupling_ids, near_held, coupling_held, transfer_held, basis_held, rows_held, links_held, raw_sems,
    id_sems, arrival_sems, near_sems, coupling_sems, small_sems, row_sems, link_sems,
):
    device = lax.axis_index("leaf") * 2 + lax.axis_index("sub")
    copy = pltpu.make_async_copy
    raw_copies = [
        copy(near_ids_in, near_raw, raw_sems.at[0]),
        copy(near_count_in, near_count, raw_sems.at[1]),
        copy(coupling_ids_in, coupling_raw, raw_sems.at[2]),
    ]
    id_copies = [copy(coupling_nodes, coupling_ids, id_sems.at[0]), copy(near_nodes, near_ids, id_sems.at[1])]
    arrivals = [
        copy(source, arrived.at[i], arrival_sems.at[i])
        for i, source in enumerate((own, near_mine, near_other, far_mine, far_other))
    ]
    small_copies = [copy(transfer, transfer_held, small_sems.at[0]), copy(basis, basis_held, small_sems.at[1])]
    places = [first + jnp.right_shift(device, t) for t, first in enumerate(FIRSTS, 1)]
    row_copies = [copy(top_transfer.at[row], rows_held.at[t], row_sems.at[t]) for t, row in enumerate(places)]
    link_copies = [copy(top_coupling.at[row], links_held.at[t], link_sems.at[t]) for t, row in enumerate(places)]
    coupling_copies = [
        copy(coupling.at[pl.ds(a, n)], coupling_held.at[pl.ds(a, n)], coupling_sems.at[i])
        for i, (a, n) in enumerate(((16, 15), (0, 16)))
    ]
    near_copies = [
        copy(near_blocks.at[pl.ds(a, 8)], near_held.at[pl.ds(a, 8)], near_sems.at[a // 8])
        for a in range(0, LEAVES, 8)
    ]
    queue = coupling_copies + near_copies
    for one in raw_copies + arrivals + queue[:1] + row_copies + link_copies + small_copies + queue[1:AHEAD]:
        one.start()

    def take(index):
        queue[index].wait()
        if index + AHEAD < len(queue):
            queue[index + AHEAD].start()

    for one in raw_copies:
        one.wait()
    near_nodes[...], coupling_nodes[...] = all_window_nodes(near_raw[...], near_count[...], coupling_raw[...])
    for one in id_copies:
        one.start()
    window[ZERO] = jnp.zeros((NV, 128), F32)
    window[ZERO + 1] = jnp.zeros((NV, 128), F32)
    for one in arrivals:
        one.wait()
    for place in range(5):
        for p in range(2 * PAIRS):
            pair = arrived[place, p].astype(F32)
            at = 2 * (place * 2 * PAIRS + p)
            window[at] = pair
            window[at + 1] = pltpu.roll(pair, K, 1)
    low = lax.broadcasted_iota(jnp.int32, (NV, 128), 1) < K

    def gathered(node, slots):
        parts = [jnp.where(low, window[node(j)], window[node(j + 1)]) for j in range(0, slots, 2)]
        return jnp.concatenate(parts, axis=1).astype(BF)

    def coupled(r):
        return dot_t(gathered(lambda j: coupling_ids[j, r], COUP), coupling_held[r])

    def near(i):
        return dot_t(gathered(lambda j: near_ids[i, j], NEAR), near_held[i])

    def descend(node, transfer_row, first):
        return dot(node.astype(BF), transfer_held[transfer_row]), beside(coupled_rows[first], coupled_rows[first + 1])

    def split(descent, added):
        top, rest = descent[:NV] + added, descent[NV:]
        return [stacked(top[:, :K], rest[:, :K]), stacked(top[:, K:], rest[:, K:])]

    def level(state, height):
        count = LEAVES >> height
        at, offset = 2 * LEAVES - 4 * count, LEAVES - 2 * count
        made = [descend(state[m], offset + m, at + 2 * m) for m in range(count)]
        return [child for one in made for child in split(*one)]

    for one in id_copies + row_copies + link_copies + small_copies:
        one.wait()
    coupled_rows = {}
    path = unit(K)
    take(0)
    for t in range(6):
        right = jnp.bitwise_and(jnp.right_shift(device, t), 1) == 1
        step = jnp.where(right, rows_held[t, :, K:], rows_held[t, :, :K])
        path = dot_t(path, step).astype(BF)
        for r in range(30 - 3 * t, max(27 - 3 * t, 15), -1):
            coupled_rows[r] = coupled(r)
        shares[:, 128 * t : 128 * t + 128] = dot(path, links_held[t]).astype(BF)
    state = [stacked(coupled_rows[30], unit(K).astype(F32))]
    take(1)
    for height in (4, 3, 2):
        state = level(state, height)
        for r in range(5 * (4 - height), 5 * (4 - height) + 5):
            coupled_rows[r] = coupled(r)
    coupled_rows[15] = coupled(15)
    take(2)
    near_rows = [near(i) for i in range(2)]
    state = level(state, 1)
    near_rows += [near(i) for i in range(2, 8)]
    ends = [dot_t(state[i].astype(BF), basis_held[i]) for i in range(LEAVES)]
    take(3)
    near_rows += [near(i) for i in range(8, LEAVES)]
    for i in range(0, LEAVES, 2):
        span = slice(K * i, K * i + 128)
        pair = beside(ends[i], ends[i + 1])
        partial[:, span] = pair[:NV] + beside(near_rows[i], near_rows[i + 1])
        onward[:, span] = pair[NV:].astype(BF)


def top_kernel(roots, transfer, ids, partial, onward, shares, potential, nodes, held_ids, sems):
    device = lax.axis_index("leaf") * 2 + lax.axis_index("sub")
    id_copy = pltpu.make_async_copy(ids, held_ids, sems.at[0])
    id_copy.start()
    low4 = lax.broadcasted_iota(jnp.int32, (4, 128), 1) < K
    made = []
    for m in range(64):
        a, b = roots[2 * m].astype(F32), roots[2 * m + 1].astype(F32)
        upper = jnp.where(low4, a, pltpu.roll(b, K, 1))
        lower = jnp.where(low4, pltpu.roll(a, K, 1), b)
        made.append(dot_t(transfer[m], stacked(upper, lower).astype(BF)).astype(BF))
    for t, first in enumerate(FIRSTS):
        if t:
            made = [
                dot(transfer[first + m], stacked(made[2 * m], made[2 * m + 1])).astype(BF)
                for m in range(len(made) // 2)
            ]
        for m, node in enumerate(made):
            nodes[first + m] = node
    id_copy.wait()
    sources = []
    for t, first in enumerate(FIRSTS, 1):
        row = first + jnp.right_shift(device, t)
        sources += [nodes[first + held_ids[0, row]], nodes[first + held_ids[1, row]]]
    incoming = dot(shares[...], stacked(*sources)).astype(BF)
    incoming = dot_t(unit(NV), incoming).astype(BF)
    potential[...] = partial[...] + dot(incoming, onward[...])


def spec(space):
    return pl.BlockSpec(memory_space=space)


VMEM, SMEM, ANY = pltpu.VMEM, pltpu.SMEM, pl.ANY


def exchanged(core, pairs):
    return [(2 * a + core, 2 * b + core) for c, d in pairs for a, b in ((c, d), (d, c))]


NEXT = (
    exchanged(0, [(c, c + 1) for c in range(2, 62, 2)])
    + exchanged(1, [(c, c + 1) for c in range(1, 62, 2)])
    + [(0, 1), (1, 2), (2, 0), (126, 127), (127, 124), (124, 126)]
)
SECOND = exchanged(0, [(c, c + 2) for c in range(64) if c % 4 < 2]) + exchanged(
    1, [(c, c + 2) for c in range(62) if c % 4 >= 2] + [(0, 1), (62, 63)]
)


def local(
    density, basis, near_ids, near_count, near_blocks, local_transfer, local_coupling, local_coupling_ids,
    top_transfer, top_coupling, top_coupling_ids,
):
    shape = jax.ShapeDtypeStruct
    pack, roots = pl.pallas_call(
        upward_kernel,
        out_shape=(shape((PAIRS, NV, 128), BF), shape((128, 4, 128), BF)),
        in_specs=[spec(VMEM)] * 3,
        out_specs=(spec(VMEM),) * 2,
        cost_estimate=pl.CostEstimate(flops=20_000_000_000, bytes_accessed=1_000_000, transcendentals=0),
        compiler_params=pltpu.CompilerParams(vmem_limit_bytes=56 << 20),
        name="upward",
    )(density, basis, local_transfer)
    every = ("leaf", "sub")
    own = lax.all_gather(pack, "sub", axis=0, tiled=True)
    near_mine = lax.ppermute(own, every, NEXT)
    far_mine = lax.ppermute(own, every, SECOND)
    all_roots = lax.all_to_all(roots, every, 0, 0, tiled=True)
    near_other = lax.ppermute(near_mine, "sub", [(0, 1), (1, 0)])
    far_other = lax.ppermute(far_mine, "sub", [(0, 1), (1, 0)])
    partial, onward, shares = pl.pallas_call(
        window_kernel,
        out_shape=(
            shape((NV, 1024), F32),
            shape((K, 1024), BF),
            shape((K, 768), BF),
        ),
        in_specs=[spec(ANY)] * 14,
        out_specs=(spec(VMEM),) * 3,
        scratch_shapes=[
            pltpu.VMEM((ZERO + 2, NV, 128), F32),
            pltpu.VMEM((5, 2 * PAIRS, NV, 128), BF),
            pltpu.VMEM((LEAVES, NEAR), jnp.int32),
            pltpu.VMEM((1, LEAVES), jnp.int32),
            pltpu.VMEM((COUP, 2 * LEAVES - 1), jnp.int32),
            pltpu.VMEM((LEAVES, NEAR), jnp.int32),
            pltpu.VMEM((COUP, 2 * LEAVES - 1), jnp.int32),
            pltpu.SMEM((LEAVES, NEAR), jnp.int32),
            pltpu.SMEM((COUP, 2 * LEAVES - 1), jnp.int32),
            pltpu.VMEM((LEAVES, 64, NEAR * 64), BF),
            pltpu.VMEM((2 * LEAVES - 1, K, COUP * K), BF),
            pltpu.VMEM((LEAVES - 1, K, 128), BF),
            pltpu.VMEM((LEAVES, 64, K), BF),
            pltpu.VMEM((6, K, 128), BF),
            pltpu.VMEM((6, K, 128), BF),
            pltpu.SemaphoreType.DMA((3,)),
            pltpu.SemaphoreType.DMA((2,)),
            pltpu.SemaphoreType.DMA((5,)),
            pltpu.SemaphoreType.DMA((4,)),
            pltpu.SemaphoreType.DMA((3,)),
            pltpu.SemaphoreType.DMA((2,)),
            pltpu.SemaphoreType.DMA((6,)),
            pltpu.SemaphoreType.DMA((6,)),
        ],
        compiler_params=pltpu.CompilerParams(vmem_limit_bytes=53 << 20),
        cost_estimate=pl.CostEstimate(flops=120_000_000, bytes_accessed=8_000_000, transcendentals=0),
        name="window",
    )(
        own, near_mine, near_other, far_mine, far_other, near_ids, near_count.reshape(1, LEAVES),
        local_coupling_ids.T, near_blocks, local_coupling, local_transfer, basis, top_transfer, top_coupling,
    )
    return pl.pallas_call(
        top_kernel,
        out_shape=shape((NV, 1024), F32),
        in_specs=[spec(VMEM)] * 2 + [spec(ANY)] + [spec(VMEM)] * 3,
        out_specs=spec(VMEM),
        scratch_shapes=[
            pltpu.VMEM((TOP, K, NV), BF),
            pltpu.SMEM((2, TOP), jnp.int32),
            pltpu.SemaphoreType.DMA((1,)),
        ],
        compiler_params=pltpu.CompilerParams(vmem_limit_bytes=20 << 20),
        name="top",
    )(all_roots, top_transfer, top_coupling_ids.T, partial, onward, shares)


def solution(mesh):
    in_specs = (
        P(None, ("leaf", "sub")),
        P(("leaf", "sub"), None, None),
        P(("leaf", "sub"), None),
        P(("leaf", "sub")),
        P(("leaf", "sub"), None, None),
        P(("leaf", "sub"), None, None),
        P(("leaf", "sub"), None, None),
        P(("leaf", "sub"), None),
        P(),
        P(),
        P(),
    )
    out_specs = P(None, ("leaf", "sub"))
    return jax.shard_map(local, mesh=mesh, in_specs=in_specs, out_specs=out_specs, check_vma=False)
```

```python
import jax
import jax.numpy as jnp
from jax import lax
from jax.experimental import pallas as pl
from jax.experimental.pallas import tpu as pltpu
from jax.sharding import PartitionSpec as P

NV = 8
K = 64
LEAVES = 16
NEAR = 24
COUP = 16
HEIGHTS = 5
PAIRS = 24
NODES = 2 * PAIRS
LEVEL_OFFSETS = (16, 32, 40, 44, 46)
ZERO = 5 * 2 * NODES
TOP = 126
AHEAD = 3
FIRSTS = (0, 64, 96, 112, 120, 124)
BF = jnp.bfloat16
F32 = jnp.float32


def dot(a, b):
    return lax.dot_general(a, b, (((1,), (0,)), ((), ())), preferred_element_type=F32)


def dot_t(a, b):
    return lax.dot_general(a, b, (((1,), (1,)), ((), ())), preferred_element_type=F32)


def unit(n):
    return (lax.broadcasted_iota(jnp.int32, (n, n), 0) == lax.broadcasted_iota(jnp.int32, (n, n), 1)).astype(BF)


def stacked(*parts):
    return jnp.concatenate(parts, axis=0)


def turned(columns):
    high = columns.astype(BF)
    rest = (columns - high.astype(F32)).astype(BF)
    return dot_t(unit(NV), high) + dot_t(unit(NV), rest)


def beside(a, b):
    return jnp.concatenate([a, b], axis=1)


def window_nodes(ids, height, offset, leaf, sub, live, slot_axis):
    shift = jnp.broadcast_to(4 - height, ids.shape)
    slot = jnp.right_shift(ids, shift)
    node = ids - jnp.left_shift(slot, shift)
    delta = jnp.right_shift(slot, 1) - 2
    core = jnp.bitwise_and(slot, 1)
    chip = leaf + delta
    odd, upper = jnp.bitwise_and(leaf, 1), jnp.bitwise_and(jnp.right_shift(leaf, 1), 1)
    place = jnp.where(delta == 1 - 2 * odd, 1 + sub, jnp.where(delta == 2 * odd - 1, 3 + sub, 0))
    place = jnp.where(delta == 2 - 4 * upper, 2 - sub, jnp.where(delta == 4 * upper - 2, 4 - sub, place))
    index = (place * 2 + core) * NODES + offset + node
    live = live & (chip >= 0) & (chip < 64)
    index = jnp.where(live, index, ZERO)
    column = lax.broadcasted_iota(jnp.int32, ids.shape, slot_axis)
    return index ^ jnp.bitwise_and(column, 1)


def all_window_nodes(near_ids, near_count, coupling_ids):
    leaf, sub = lax.axis_index("leaf"), lax.axis_index("sub")
    slots = lax.broadcasted_iota(jnp.int32, near_ids.shape, 1)
    diagonal = lax.broadcasted_iota(jnp.int32, (LEAVES, LEAVES), 0) == lax.broadcasted_iota(
        jnp.int32, (LEAVES, LEAVES), 1
    )
    counts = jnp.sum(jnp.where(diagonal, near_count, 0), axis=1, keepdims=True)
    near_nodes = window_nodes(near_ids, 0, 0, leaf, sub, slots < counts, 1)
    rows = lax.broadcasted_iota(jnp.int32, coupling_ids.shape, 1)
    height = sum((rows >= 2 * LEAVES - 2 * (LEAVES >> h)).astype(jnp.int32) for h in range(1, HEIGHTS))
    offset = jnp.zeros(coupling_ids.shape, jnp.int32)
    for h, place in enumerate(LEVEL_OFFSETS):
        offset = jnp.where(height == h, place, offset)
    coupling_nodes = window_nodes(coupling_ids, height, offset, leaf, sub, coupling_ids >= 0, 0)
    return near_nodes, coupling_nodes


def upward_kernel(density, basis, transfer, pack, roots):
    level = []
    for p in range(8):
        pair = density[:, 128 * p : 128 * p + 128]
        pack[p] = pair
        joined = beside(dot(pair[:, :K], basis[2 * p]), dot(pair[:, K:], basis[2 * p + 1])).astype(BF)
        pack[8 + p] = joined
        level.append(joined)
    made = [dot_t(transfer[m], pair).astype(BF) for m, pair in enumerate(level)]
    columns, first = list(made), 8
    while len(made) > 1:
        made = [
            dot(transfer[first + q], stacked(made[2 * q], made[2 * q + 1])).astype(BF)
            for q in range(len(made) // 2)
        ]
        first += len(made)
        columns += made
    rows = dot_t(unit(NV), stacked(*columns))
    for q in range(7):
        pack[16 + q] = rows[:, 128 * q : 128 * q + 128].astype(BF)
    root = rows[:, 896:]
    pack[23] = beside(root, root).astype(BF)
    sent = beside(root[:4], root[4:]).astype(BF)
    roots[...] = jnp.broadcast_to(sent[None], roots.shape)


def window_kernel(
    own, inner_mine, inner_other, outer_mine, outer_other, near_ids_in, near_count_in, coupling_ids_in, near_blocks,
    coupling, transfer, basis, top_transfer, top_coupling, partial, onward, shares, window, arrived, near_raw,
    near_count, coupling_raw, near_nodes, coupling_nodes, near_ids, coupling_ids, near_held, coupling_held, transfer_held, basis_held, rows_held, links_held, raw_sems,
    id_sems, arrival_sems, near_sems, coupling_sems, small_sems, row_sems, link_sems,
):
    device = lax.axis_index("leaf") * 2 + lax.axis_index("sub")
    copy = pltpu.make_async_copy
    raw_copies = [
        copy(near_ids_in, near_raw, raw_sems.at[0]),
        copy(near_count_in, near_count, raw_sems.at[1]),
        copy(coupling_ids_in, coupling_raw, raw_sems.at[2]),
    ]
    id_copies = [copy(coupling_nodes, coupling_ids, id_sems.at[0]), copy(near_nodes, near_ids, id_sems.at[1])]
    arrivals = [
        copy(source, arrived.at[i], arrival_sems.at[i])
        for i, source in enumerate((own, inner_mine, inner_other, outer_mine, outer_other))
    ]
    small_copies = [copy(transfer, transfer_held, small_sems.at[0]), copy(basis, basis_held, small_sems.at[1])]
    places = [first + jnp.right_shift(device, t) for t, first in enumerate(FIRSTS, 1)]
    row_copies = [copy(top_transfer.at[row], rows_held.at[t], row_sems.at[t]) for t, row in enumerate(places)]
    link_copies = [copy(top_coupling.at[row], links_held.at[t], link_sems.at[t]) for t, row in enumerate(places)]
    coupling_copies = [
        copy(coupling.at[pl.ds(a, n)], coupling_held.at[pl.ds(a, n)], coupling_sems.at[i])
        for i, (a, n) in enumerate(((16, 15), (0, 16)))
    ]
    near_copies = [
        copy(near_blocks.at[pl.ds(a, 8)], near_held.at[pl.ds(a, 8)], near_sems.at[a // 8])
        for a in range(0, LEAVES, 8)
    ]
    queue = coupling_copies + near_copies
    for one in raw_copies + arrivals + queue[:1] + row_copies + link_copies + small_copies + queue[1:AHEAD]:
        one.start()

    def take(index):
        queue[index].wait()
        if index + AHEAD < len(queue):
            queue[index + AHEAD].start()

    for one in raw_copies:
        one.wait()
    near_nodes[...], coupling_nodes[...] = all_window_nodes(near_raw[...], near_count[...], coupling_raw[...])
    for one in id_copies:
        one.start()
    window[ZERO] = jnp.zeros((NV, 128), F32)
    window[ZERO + 1] = jnp.zeros((NV, 128), F32)
    for one in arrivals:
        one.wait()
    for place in range(5):
        for p in range(2 * PAIRS):
            pair = arrived[place, p].astype(F32)
            at = 2 * (place * 2 * PAIRS + p)
            window[at] = pair
            window[at + 1] = pltpu.roll(pair, K, 1)
    low = lax.broadcasted_iota(jnp.int32, (NV, 128), 1) < K

    def gathered(node, slots):
        parts = [jnp.where(low, window[node(j)], window[node(j + 1)]) for j in range(0, slots, 2)]
        return jnp.concatenate(parts, axis=1).astype(BF)

    def coupled(r):
        return dot_t(gathered(lambda j: coupling_ids[j, r], COUP), coupling_held[r])

    def near(i):
        return dot_t(gathered(lambda j: near_ids[i, j], NEAR), near_held[i])

    def descend(node, transfer_row, first):
        return dot(node.astype(BF), transfer_held[transfer_row]), beside(coupled_rows[first], coupled_rows[first + 1])

    def split(descent, added):
        top, rest = descent[:NV] + added, descent[NV:]
        return [stacked(top[:, :K], rest[:, :K]), stacked(top[:, K:], rest[:, K:])]

    def level(state, height):
        count = LEAVES >> height
        at, offset = 2 * LEAVES - 4 * count, LEAVES - 2 * count
        made = [descend(state[m], offset + m, at + 2 * m) for m in range(count)]
        return [child for one in made for child in split(*one)]

    for one in id_copies + row_copies + link_copies + small_copies:
        one.wait()
    coupled_rows = {}
    path = unit(K)
    take(0)
    for t in range(6):
        right = jnp.bitwise_and(jnp.right_shift(device, t), 1) == 1
        step = jnp.where(right, rows_held[t, :, K:], rows_held[t, :, :K])
        path = dot_t(path, step).astype(BF)
        for r in range(30 - 3 * t, max(27 - 3 * t, 15), -1):
            coupled_rows[r] = coupled(r)
        shares[:, 128 * t : 128 * t + 128] = dot(path, links_held[t]).astype(BF)
    state = [stacked(coupled_rows[30], unit(K).astype(F32))]
    take(1)
    for height in (4, 3, 2):
        state = level(state, height)
        for r in range(5 * (4 - height), 5 * (4 - height) + 5):
            coupled_rows[r] = coupled(r)
    coupled_rows[15] = coupled(15)
    take(2)
    near_rows = [near(i) for i in range(2)]
    state = level(state, 1)
    near_rows += [near(i) for i in range(2, 8)]
    ends = [dot_t(state[i].astype(BF), basis_held[i]) for i in range(LEAVES)]
    take(3)
    near_rows += [near(i) for i in range(8, LEAVES)]
    for i in range(0, LEAVES, 2):
        span = slice(K * i, K * i + 128)
        pair = beside(ends[i], ends[i + 1])
        partial[:, span] = pair[:NV] + beside(near_rows[i], near_rows[i + 1])
        onward[:, span] = pair[NV:].astype(BF)


def top_kernel(roots, transfer, ids, partial, onward, shares, potential, nodes, held_ids, sems):
    device = lax.axis_index("leaf") * 2 + lax.axis_index("sub")
    id_copy = pltpu.make_async_copy(ids, held_ids, sems.at[0])
    id_copy.start()
    low4 = lax.broadcasted_iota(jnp.int32, (4, 128), 1) < K
    made = []
    for m in range(64):
        a, b = roots[2 * m].astype(F32), roots[2 * m + 1].astype(F32)
        upper = jnp.where(low4, a, pltpu.roll(b, K, 1))
        lower = jnp.where(low4, pltpu.roll(a, K, 1), b)
        made.append(dot_t(transfer[m], stacked(upper, lower).astype(BF)).astype(BF))
    for t, first in enumerate(FIRSTS):
        if t:
            made = [
                dot(transfer[first + m], stacked(made[2 * m], made[2 * m + 1])).astype(BF)
                for m in range(len(made) // 2)
            ]
        for m, node in enumerate(made):
            nodes[first + m] = node
    id_copy.wait()
    sources = []
    for t, first in enumerate(FIRSTS, 1):
        row = first + jnp.right_shift(device, t)
        sources += [nodes[first + held_ids[0, row]], nodes[first + held_ids[1, row]]]
    incoming = dot(shares[...], stacked(*sources)).astype(BF)
    incoming = dot_t(unit(NV), incoming).astype(BF)
    potential[...] = partial[...] + dot(incoming, onward[...])


def spec(space):
    return pl.BlockSpec(memory_space=space)


VMEM, SMEM, ANY = pltpu.VMEM, pltpu.SMEM, pl.ANY


def exchanged(core, pairs):
    return [(2 * a + core, 2 * b + core) for c, d in pairs for a, b in ((c, d), (d, c))]


INNER = exchanged(0, [(c, c + 1) for c in range(0, 64, 2)]) + exchanged(
    1, [(c, c + 2) for c in range(64) if c % 4 < 2]
)
OUTER = (
    exchanged(0, [(c, c + 1) for c in range(1, 63, 2)])
    + exchanged(1, [(c, c + 2) for c in range(62) if c % 4 >= 2])
    + [(0, 1), (1, 3), (3, 0), (126, 127), (127, 125), (125, 126)]
)


def local(
    density, basis, near_ids, near_count, near_blocks, local_transfer, local_coupling, local_coupling_ids,
    top_transfer, top_coupling, top_coupling_ids,
):
    shape = jax.ShapeDtypeStruct
    pack, roots = pl.pallas_call(
        upward_kernel,
        out_shape=(shape((PAIRS, NV, 128), BF), shape((128, 4, 128), BF)),
        in_specs=[spec(VMEM)] * 3,
        out_specs=(spec(VMEM),) * 2,
        cost_estimate=pl.CostEstimate(flops=20_000_000_000, bytes_accessed=1_000_000, transcendentals=0),
        compiler_params=pltpu.CompilerParams(vmem_limit_bytes=56 << 20),
        name="upward",
    )(density, basis, local_transfer)
    every = ("leaf", "sub")
    own = lax.all_gather(pack, "sub", axis=0, tiled=True)
    inner_mine = lax.ppermute(own, every, INNER)
    outer_mine = lax.ppermute(own, every, OUTER)
    all_roots = lax.all_to_all(roots, every, 0, 0, tiled=True)
    inner_other = lax.ppermute(inner_mine, "sub", [(0, 1), (1, 0)])
    outer_other = lax.ppermute(outer_mine, "sub", [(0, 1), (1, 0)])
    partial, onward, shares = pl.pallas_call(
        window_kernel,
        out_shape=(
            shape((NV, 1024), F32),
            shape((K, 1024), BF),
            shape((K, 768), BF),
        ),
        in_specs=[spec(ANY)] * 14,
        out_specs=(spec(VMEM),) * 3,
        scratch_shapes=[
            pltpu.VMEM((ZERO + 2, NV, 128), F32),
            pltpu.VMEM((5, 2 * PAIRS, NV, 128), BF),
            pltpu.VMEM((LEAVES, NEAR), jnp.int32),
            pltpu.VMEM((1, LEAVES), jnp.int32),
            pltpu.VMEM((COUP, 2 * LEAVES - 1), jnp.int32),
            pltpu.VMEM((LEAVES, NEAR), jnp.int32),
            pltpu.VMEM((COUP, 2 * LEAVES - 1), jnp.int32),
            pltpu.SMEM((LEAVES, NEAR), jnp.int32),
            pltpu.SMEM((COUP, 2 * LEAVES - 1), jnp.int32),
            pltpu.VMEM((LEAVES, 64, NEAR * 64), BF),
            pltpu.VMEM((2 * LEAVES - 1, K, COUP * K), BF),
            pltpu.VMEM((LEAVES - 1, K, 128), BF),
            pltpu.VMEM((LEAVES, 64, K), BF),
            pltpu.VMEM((6, K, 128), BF),
            pltpu.VMEM((6, K, 128), BF),
            pltpu.SemaphoreType.DMA((3,)),
            pltpu.SemaphoreType.DMA((2,)),
            pltpu.SemaphoreType.DMA((5,)),
            pltpu.SemaphoreType.DMA((4,)),
            pltpu.SemaphoreType.DMA((3,)),
            pltpu.SemaphoreType.DMA((2,)),
            pltpu.SemaphoreType.DMA((6,)),
            pltpu.SemaphoreType.DMA((6,)),
        ],
        compiler_params=pltpu.CompilerParams(vmem_limit_bytes=53 << 20),
        cost_estimate=pl.CostEstimate(flops=120_000_000, bytes_accessed=8_000_000, transcendentals=0),
        name="window",
    )(
        own, inner_mine, inner_other, outer_mine, outer_other, near_ids, near_count.reshape(1, LEAVES),
        local_coupling_ids.T, near_blocks, local_coupling, local_transfer, basis, top_transfer, top_coupling,
    )
    return pl.pallas_call(
        top_kernel,
        out_shape=shape((NV, 1024), F32),
        in_specs=[spec(VMEM)] * 2 + [spec(ANY)] + [spec(VMEM)] * 3,
        out_specs=spec(VMEM),
        scratch_shapes=[
            pltpu.VMEM((TOP, K, NV), BF),
            pltpu.SMEM((2, TOP), jnp.int32),
            pltpu.SemaphoreType.DMA((1,)),
        ],
        compiler_params=pltpu.CompilerParams(vmem_limit_bytes=20 << 20),
        name="top",
    )(all_roots, top_transfer, top_coupling_ids.T, partial, onward, shares)


def solution(mesh):
    in_specs = (
        P(None, ("leaf", "sub")),
        P(("leaf", "sub"), None, None),
        P(("leaf", "sub"), None),
        P(("leaf", "sub")),
        P(("leaf", "sub"), None, None),
        P(("leaf", "sub"), None, None),
        P(("leaf", "sub"), None, None),
        P(("leaf", "sub"), None),
        P(),
        P(),
        P(),
    )
    out_specs = P(None, ("leaf", "sub"))
    return jax.shard_map(local, mesh=mesh, in_specs=in_specs, out_specs=out_specs, check_vma=False)
```

```python
import jax
import jax.numpy as jnp
from jax import lax
from jax.experimental import pallas as pl
from jax.experimental.pallas import tpu as pltpu
from jax.sharding import PartitionSpec as P

NV = 8
K = 64
LEAVES = 16
NEAR = 24
COUP = 16
HEIGHTS = 5
PAIRS = 24
NODES = 2 * PAIRS
LEVEL_OFFSETS = (16, 32, 40, 44, 46)
ZERO = 5 * 2 * NODES
TOP = 126
AHEAD = 3
FIRSTS = (0, 64, 96, 112, 120, 124)
BF = jnp.bfloat16
F32 = jnp.float32


def dot(a, b):
    return lax.dot_general(a, b, (((1,), (0,)), ((), ())), preferred_element_type=F32)


def dot_t(a, b):
    return lax.dot_general(a, b, (((1,), (1,)), ((), ())), preferred_element_type=F32)


def unit(n):
    return (lax.broadcasted_iota(jnp.int32, (n, n), 0) == lax.broadcasted_iota(jnp.int32, (n, n), 1)).astype(BF)


def stacked(*parts):
    return jnp.concatenate(parts, axis=0)


def turned(columns):
    high = columns.astype(BF)
    rest = (columns - high.astype(F32)).astype(BF)
    return dot_t(unit(NV), high) + dot_t(unit(NV), rest)


def beside(a, b):
    return jnp.concatenate([a, b], axis=1)


def window_nodes(ids, height, offset, leaf, sub, live, slot_axis):
    shift = jnp.broadcast_to(4 - height, ids.shape)
    slot = jnp.right_shift(ids, shift)
    node = ids - jnp.left_shift(slot, shift)
    delta = jnp.right_shift(slot, 1) - 2
    core = jnp.bitwise_and(slot, 1)
    chip = leaf + delta
    odd, upper = jnp.bitwise_and(leaf, 1), jnp.bitwise_and(jnp.right_shift(leaf, 1), 1)
    place = jnp.where(delta == 1 - 2 * odd, 1 + sub, jnp.where(delta == 2 * odd - 1, 3 + sub, 0))
    place = jnp.where(delta == 2 - 4 * upper, 2 - sub, jnp.where(delta == 4 * upper - 2, 4 - sub, place))
    second = core ^ sub ^ ((place == 2) | (place == 4)).astype(jnp.int32)
    index = (place * 2 + second) * NODES + offset + node
    live = live & (chip >= 0) & (chip < 64)
    index = jnp.where(live, index, ZERO)
    column = lax.broadcasted_iota(jnp.int32, ids.shape, slot_axis)
    return index ^ jnp.bitwise_and(column, 1)


def all_window_nodes(near_ids, near_count, coupling_ids):
    leaf, sub = lax.axis_index("leaf"), lax.axis_index("sub")
    slots = lax.broadcasted_iota(jnp.int32, near_ids.shape, 1)
    diagonal = lax.broadcasted_iota(jnp.int32, (LEAVES, LEAVES), 0) == lax.broadcasted_iota(
        jnp.int32, (LEAVES, LEAVES), 1
    )
    counts = jnp.sum(jnp.where(diagonal, near_count, 0), axis=1, keepdims=True)
    near_nodes = window_nodes(near_ids, 0, 0, leaf, sub, slots < counts, 1)
    rows = lax.broadcasted_iota(jnp.int32, coupling_ids.shape, 1)
    height = sum((rows >= 2 * LEAVES - 2 * (LEAVES >> h)).astype(jnp.int32) for h in range(1, HEIGHTS))
    offset = jnp.zeros(coupling_ids.shape, jnp.int32)
    for h, place in enumerate(LEVEL_OFFSETS):
        offset = jnp.where(height == h, place, offset)
    coupling_nodes = window_nodes(coupling_ids, height, offset, leaf, sub, coupling_ids >= 0, 0)
    return near_nodes, coupling_nodes


def upward_kernel(density, basis, transfer, pack, roots):
    level = []
    for p in range(8):
        pair = density[:, 128 * p : 128 * p + 128]
        pack[p] = pair
        joined = beside(dot(pair[:, :K], basis[2 * p]), dot(pair[:, K:], basis[2 * p + 1])).astype(BF)
        pack[8 + p] = joined
        level.append(joined)
    made = [dot_t(transfer[m], pair).astype(BF) for m, pair in enumerate(level)]
    columns, first = list(made), 8
    while len(made) > 1:
        made = [
            dot(transfer[first + q], stacked(made[2 * q], made[2 * q + 1])).astype(BF)
            for q in range(len(made) // 2)
        ]
        first += len(made)
        columns += made
    rows = dot_t(unit(NV), stacked(*columns))
    for q in range(7):
        pack[16 + q] = rows[:, 128 * q : 128 * q + 128].astype(BF)
    root = rows[:, 896:]
    pack[23] = beside(root, root).astype(BF)
    sent = beside(root[:4], root[4:]).astype(BF)
    roots[...] = jnp.broadcast_to(sent[None], roots.shape)


def window_kernel(
    own, inner_mine, inner_other, outer_mine, outer_other, near_ids_in, near_count_in, coupling_ids_in, near_blocks,
    coupling, transfer, basis, top_transfer, top_coupling, partial, onward, shares, window, arrived, near_raw,
    near_count, coupling_raw, near_nodes, coupling_nodes, near_ids, coupling_ids, near_held, coupling_held, transfer_held, basis_held, rows_held, links_held, raw_sems,
    id_sems, arrival_sems, near_sems, coupling_sems, small_sems, row_sems, link_sems,
):
    device = lax.axis_index("leaf") * 2 + lax.axis_index("sub")
    copy = pltpu.make_async_copy
    raw_copies = [
        copy(near_ids_in, near_raw, raw_sems.at[0]),
        copy(near_count_in, near_count, raw_sems.at[1]),
        copy(coupling_ids_in, coupling_raw, raw_sems.at[2]),
    ]
    id_copies = [copy(coupling_nodes, coupling_ids, id_sems.at[0]), copy(near_nodes, near_ids, id_sems.at[1])]
    arrivals = [
        copy(source, arrived.at[i], arrival_sems.at[i])
        for i, source in enumerate((own, inner_mine, inner_other, outer_mine, outer_other))
    ]
    small_copies = [copy(transfer, transfer_held, small_sems.at[0]), copy(basis, basis_held, small_sems.at[1])]
    places = [first + jnp.right_shift(device, t) for t, first in enumerate(FIRSTS, 1)]
    row_copies = [copy(top_transfer.at[row], rows_held.at[t], row_sems.at[t]) for t, row in enumerate(places)]
    link_copies = [copy(top_coupling.at[row], links_held.at[t], link_sems.at[t]) for t, row in enumerate(places)]
    coupling_copies = [
        copy(coupling.at[pl.ds(a, n)], coupling_held.at[pl.ds(a, n)], coupling_sems.at[i])
        for i, (a, n) in enumerate(((16, 15), (0, 16)))
    ]
    near_copies = [
        copy(near_blocks.at[pl.ds(a, 8)], near_held.at[pl.ds(a, 8)], near_sems.at[a // 8])
        for a in range(0, LEAVES, 8)
    ]
    queue = coupling_copies + near_copies
    for one in raw_copies + arrivals + queue[:1] + row_copies + link_copies + small_copies + queue[1:AHEAD]:
        one.start()

    def take(index):
        queue[index].wait()
        if index + AHEAD < len(queue):
            queue[index + AHEAD].start()

    for one in raw_copies:
        one.wait()
    near_nodes[...], coupling_nodes[...] = all_window_nodes(near_raw[...], near_count[...], coupling_raw[...])
    for one in id_copies:
        one.start()
    window[ZERO] = jnp.zeros((NV, 128), F32)
    window[ZERO + 1] = jnp.zeros((NV, 128), F32)
    for one in arrivals:
        one.wait()
    for place in range(5):
        for p in range(2 * PAIRS):
            pair = arrived[place, p].astype(F32)
            at = 2 * (place * 2 * PAIRS + p)
            window[at] = pair
            window[at + 1] = pltpu.roll(pair, K, 1)
    low = lax.broadcasted_iota(jnp.int32, (NV, 128), 1) < K

    def gathered(node, slots):
        parts = [jnp.where(low, window[node(j)], window[node(j + 1)]) for j in range(0, slots, 2)]
        return jnp.concatenate(parts, axis=1).astype(BF)

    def coupled(r):
        return dot_t(gathered(lambda j: coupling_ids[j, r], COUP), coupling_held[r])

    def near(i):
        return dot_t(gathered(lambda j: near_ids[i, j], NEAR), near_held[i])

    def descend(node, transfer_row, first):
        return dot(node.astype(BF), transfer_held[transfer_row]), beside(coupled_rows[first], coupled_rows[first + 1])

    def split(descent, added):
        top, rest = descent[:NV] + added, descent[NV:]
        return [stacked(top[:, :K], rest[:, :K]), stacked(top[:, K:], rest[:, K:])]

    def level(state, height):
        count = LEAVES >> height
        at, offset = 2 * LEAVES - 4 * count, LEAVES - 2 * count
        made = [descend(state[m], offset + m, at + 2 * m) for m in range(count)]
        return [child for one in made for child in split(*one)]

    for one in id_copies + row_copies + link_copies + small_copies:
        one.wait()
    coupled_rows = {}
    path = unit(K)
    take(0)
    for t in range(6):
        right = jnp.bitwise_and(jnp.right_shift(device, t), 1) == 1
        step = jnp.where(right, rows_held[t, :, K:], rows_held[t, :, :K])
        path = dot_t(path, step).astype(BF)
        for r in range(30 - 3 * t, max(27 - 3 * t, 15), -1):
            coupled_rows[r] = coupled(r)
        shares[:, 128 * t : 128 * t + 128] = dot(path, links_held[t]).astype(BF)
    state = [stacked(coupled_rows[30], unit(K).astype(F32))]
    take(1)
    for height in (4, 3, 2):
        state = level(state, height)
        for r in range(5 * (4 - height), 5 * (4 - height) + 5):
            coupled_rows[r] = coupled(r)
    coupled_rows[15] = coupled(15)
    take(2)
    near_rows = [near(i) for i in range(2)]
    state = level(state, 1)
    near_rows += [near(i) for i in range(2, 8)]
    ends = [dot_t(state[i].astype(BF), basis_held[i]) for i in range(LEAVES)]
    take(3)
    near_rows += [near(i) for i in range(8, LEAVES)]
    for i in range(0, LEAVES, 2):
        span = slice(K * i, K * i + 128)
        pair = beside(ends[i], ends[i + 1])
        partial[:, span] = pair[:NV] + beside(near_rows[i], near_rows[i + 1])
        onward[:, span] = pair[NV:].astype(BF)


def top_kernel(roots, transfer, ids, partial, onward, shares, potential, nodes, held_ids, sems):
    device = lax.axis_index("leaf") * 2 + lax.axis_index("sub")
    id_copy = pltpu.make_async_copy(ids, held_ids, sems.at[0])
    id_copy.start()
    low4 = lax.broadcasted_iota(jnp.int32, (4, 128), 1) < K
    made = []
    for m in range(64):
        a, b = roots[2 * m].astype(F32), roots[2 * m + 1].astype(F32)
        upper = jnp.where(low4, a, pltpu.roll(b, K, 1))
        lower = jnp.where(low4, pltpu.roll(a, K, 1), b)
        made.append(dot_t(transfer[m], stacked(upper, lower).astype(BF)).astype(BF))
    for t, first in enumerate(FIRSTS):
        if t:
            made = [
                dot(transfer[first + m], stacked(made[2 * m], made[2 * m + 1])).astype(BF)
                for m in range(len(made) // 2)
            ]
        for m, node in enumerate(made):
            nodes[first + m] = node
    id_copy.wait()
    sources = []
    for t, first in enumerate(FIRSTS, 1):
        row = first + jnp.right_shift(device, t)
        sources += [nodes[first + held_ids[0, row]], nodes[first + held_ids[1, row]]]
    incoming = dot(shares[...], stacked(*sources)).astype(BF)
    incoming = dot_t(unit(NV), incoming).astype(BF)
    potential[...] = partial[...] + dot(incoming, onward[...])


def spec(space):
    return pl.BlockSpec(memory_space=space)


VMEM, SMEM, ANY = pltpu.VMEM, pltpu.SMEM, pl.ANY


def exchanged(core, pairs):
    return [(2 * a + core, 2 * b + core) for c, d in pairs for a, b in ((c, d), (d, c))]


INNER = exchanged(0, [(c, c + 1) for c in range(0, 64, 2)]) + exchanged(
    1, [(c, c + 2) for c in range(64) if c % 4 < 2]
)
OUTER = (
    exchanged(0, [(c, c + 1) for c in range(1, 63, 2)])
    + exchanged(1, [(c, c + 2) for c in range(62) if c % 4 >= 2])
    + [(0, 1), (1, 3), (3, 0), (126, 127), (127, 125), (125, 126)]
)


def local(
    density, basis, near_ids, near_count, near_blocks, local_transfer, local_coupling, local_coupling_ids,
    top_transfer, top_coupling, top_coupling_ids,
):
    shape = jax.ShapeDtypeStruct
    pack, roots = pl.pallas_call(
        upward_kernel,
        out_shape=(shape((PAIRS, NV, 128), BF), shape((128, 4, 128), BF)),
        in_specs=[spec(VMEM)] * 3,
        out_specs=(spec(VMEM),) * 2,
        cost_estimate=pl.CostEstimate(flops=20_000_000_000, bytes_accessed=1_000_000, transcendentals=0),
        compiler_params=pltpu.CompilerParams(vmem_limit_bytes=56 << 20),
        name="upward",
    )(density, basis, local_transfer)
    every = ("leaf", "sub")
    own = jnp.concatenate([pack, lax.ppermute(pack, "sub", [(0, 1), (1, 0)])])
    inner_mine = lax.ppermute(own, every, INNER)
    outer_mine = lax.ppermute(own, every, OUTER)
    all_roots = lax.all_to_all(roots, every, 0, 0, tiled=True)
    inner_other = lax.ppermute(inner_mine, "sub", [(0, 1), (1, 0)])
    outer_other = lax.ppermute(outer_mine, "sub", [(0, 1), (1, 0)])
    partial, onward, shares = pl.pallas_call(
        window_kernel,
        out_shape=(
            shape((NV, 1024), F32),
            shape((K, 1024), BF),
            shape((K, 768), BF),
        ),
        in_specs=[spec(ANY)] * 14,
        out_specs=(spec(VMEM),) * 3,
        scratch_shapes=[
            pltpu.VMEM((ZERO + 2, NV, 128), F32),
            pltpu.VMEM((5, 2 * PAIRS, NV, 128), BF),
            pltpu.VMEM((LEAVES, NEAR), jnp.int32),
            pltpu.VMEM((1, LEAVES), jnp.int32),
            pltpu.VMEM((COUP, 2 * LEAVES - 1), jnp.int32),
            pltpu.VMEM((LEAVES, NEAR), jnp.int32),
            pltpu.VMEM((COUP, 2 * LEAVES - 1), jnp.int32),
            pltpu.SMEM((LEAVES, NEAR), jnp.int32),
            pltpu.SMEM((COUP, 2 * LEAVES - 1), jnp.int32),
            pltpu.VMEM((LEAVES, 64, NEAR * 64), BF),
            pltpu.VMEM((2 * LEAVES - 1, K, COUP * K), BF),
            pltpu.VMEM((LEAVES - 1, K, 128), BF),
            pltpu.VMEM((LEAVES, 64, K), BF),
            pltpu.VMEM((6, K, 128), BF),
            pltpu.VMEM((6, K, 128), BF),
            pltpu.SemaphoreType.DMA((3,)),
            pltpu.SemaphoreType.DMA((2,)),
            pltpu.SemaphoreType.DMA((5,)),
            pltpu.SemaphoreType.DMA((4,)),
            pltpu.SemaphoreType.DMA((3,)),
            pltpu.SemaphoreType.DMA((2,)),
            pltpu.SemaphoreType.DMA((6,)),
            pltpu.SemaphoreType.DMA((6,)),
        ],
        compiler_params=pltpu.CompilerParams(vmem_limit_bytes=53 << 20),
        cost_estimate=pl.CostEstimate(flops=120_000_000, bytes_accessed=8_000_000, transcendentals=0),
        name="window",
    )(
        own, inner_mine, inner_other, outer_mine, outer_other, near_ids, near_count.reshape(1, LEAVES),
        local_coupling_ids.T, near_blocks, local_coupling, local_transfer, basis, top_transfer, top_coupling,
    )
    return pl.pallas_call(
        top_kernel,
        out_shape=shape((NV, 1024), F32),
        in_specs=[spec(VMEM)] * 2 + [spec(ANY)] + [spec(VMEM)] * 3,
        out_specs=spec(VMEM),
        scratch_shapes=[
            pltpu.VMEM((TOP, K, NV), BF),
            pltpu.SMEM((2, TOP), jnp.int32),
            pltpu.SemaphoreType.DMA((1,)),
        ],
        compiler_params=pltpu.CompilerParams(vmem_limit_bytes=20 << 20),
        name="top",
    )(all_roots, top_transfer, top_coupling_ids.T, partial, onward, shares)


def solution(mesh):
    in_specs = (
        P(None, ("leaf", "sub")),
        P(("leaf", "sub"), None, None),
        P(("leaf", "sub"), None),
        P(("leaf", "sub")),
        P(("leaf", "sub"), None, None),
        P(("leaf", "sub"), None, None),
        P(("leaf", "sub"), None, None),
        P(("leaf", "sub"), None),
        P(),
        P(),
        P(),
    )
    out_specs = P(None, ("leaf", "sub"))
    return jax.shard_map(local, mesh=mesh, in_specs=in_specs, out_specs=out_specs, check_vma=False)
```

```python
import jax
import jax.numpy as jnp
from jax import lax
from jax.experimental import pallas as pl
from jax.experimental.pallas import tpu as pltpu
from jax.sharding import PartitionSpec as P

NV = 8
K = 64
LEAVES = 16
NEAR = 24
COUP = 16
HEIGHTS = 5
PAIRS = 24
NODES = 2 * PAIRS
LEVEL_OFFSETS = (16, 32, 40, 44, 46)
ZERO = 5 * 2 * NODES
TOP = 126
AHEAD = 3
FIRSTS = (0, 64, 96, 112, 120, 124)
BF = jnp.bfloat16
F32 = jnp.float32


def dot(a, b):
    return lax.dot_general(a, b, (((1,), (0,)), ((), ())), preferred_element_type=F32)


def dot_t(a, b):
    return lax.dot_general(a, b, (((1,), (1,)), ((), ())), preferred_element_type=F32)


def unit(n):
    return (lax.broadcasted_iota(jnp.int32, (n, n), 0) == lax.broadcasted_iota(jnp.int32, (n, n), 1)).astype(BF)


def stacked(*parts):
    return jnp.concatenate(parts, axis=0)


def turned(columns):
    high = columns.astype(BF)
    rest = (columns - high.astype(F32)).astype(BF)
    return dot_t(unit(NV), high) + dot_t(unit(NV), rest)


def beside(a, b):
    return jnp.concatenate([a, b], axis=1)


def window_nodes(ids, height, offset, leaf, sub, live, slot_axis):
    shift = jnp.broadcast_to(4 - height, ids.shape)
    slot = jnp.right_shift(ids, shift)
    node = ids - jnp.left_shift(slot, shift)
    delta = jnp.right_shift(slot, 1) - 2
    core = jnp.bitwise_and(slot, 1)
    chip = leaf + delta
    odd, upper = jnp.bitwise_and(leaf, 1), jnp.bitwise_and(jnp.right_shift(leaf, 1), 1)
    place = jnp.where(delta == 1 - 2 * odd, 1 + sub, jnp.where(delta == 2 * odd - 1, 3 + sub, 0))
    place = jnp.where(delta == 2 - 4 * upper, 2 - sub, jnp.where(delta == 4 * upper - 2, 4 - sub, place))
    second = core ^ sub ^ ((place == 2) | (place == 4)).astype(jnp.int32)
    index = (place * 2 + second) * NODES + offset + node
    live = live & (chip >= 0) & (chip < 64)
    index = jnp.where(live, index, ZERO)
    column = lax.broadcasted_iota(jnp.int32, ids.shape, slot_axis)
    return index ^ jnp.bitwise_and(column, 1)


def all_window_nodes(near_ids, near_count, coupling_ids):
    leaf, sub = lax.axis_index("leaf"), lax.axis_index("sub")
    slots = lax.broadcasted_iota(jnp.int32, near_ids.shape, 1)
    diagonal = lax.broadcasted_iota(jnp.int32, (LEAVES, LEAVES), 0) == lax.broadcasted_iota(
        jnp.int32, (LEAVES, LEAVES), 1
    )
    counts = jnp.sum(jnp.where(diagonal, near_count, 0), axis=1, keepdims=True)
    near_nodes = window_nodes(near_ids, 0, 0, leaf, sub, slots < counts, 1)
    rows = lax.broadcasted_iota(jnp.int32, coupling_ids.shape, 1)
    height = sum((rows >= 2 * LEAVES - 2 * (LEAVES >> h)).astype(jnp.int32) for h in range(1, HEIGHTS))
    offset = jnp.zeros(coupling_ids.shape, jnp.int32)
    for h, place in enumerate(LEVEL_OFFSETS):
        offset = jnp.where(height == h, place, offset)
    coupling_nodes = window_nodes(coupling_ids, height, offset, leaf, sub, coupling_ids >= 0, 0)
    return near_nodes, coupling_nodes


def upward_kernel(density, basis, transfer, pack, roots):
    level = []
    for p in range(8):
        pair = density[:, 128 * p : 128 * p + 128]
        pack[p] = pair
        joined = beside(dot(pair[:, :K], basis[2 * p]), dot(pair[:, K:], basis[2 * p + 1])).astype(BF)
        pack[8 + p] = joined
        level.append(joined)
    grand = [
        beside(
            dot(transfer[8 + q, :, :K], transfer[2 * q]).astype(BF),
            dot(transfer[8 + q, :, K:], transfer[2 * q + 1]).astype(BF),
        )
        for q in range(4)
    ]
    root_map = beside(
        dot(transfer[14, :, :K], transfer[12]).astype(BF), dot(transfer[14, :, K:], transfer[13]).astype(BF)
    )
    second = [dot_t(grand[q], beside(level[2 * q], level[2 * q + 1])).astype(BF) for q in range(4)]
    first = [dot_t(transfer[m], pair).astype(BF) for m, pair in enumerate(level)]
    top = dot(root_map, stacked(*second)).astype(BF)
    third = [dot(transfer[12 + q], stacked(second[2 * q], second[2 * q + 1])).astype(BF) for q in range(2)]
    rows = stacked(*first, *second, *third, top).astype(F32).T
    for q in range(7):
        pack[16 + q] = rows[:, 128 * q : 128 * q + 128].astype(BF)
    root = rows[:, 896:]
    pack[23] = beside(root, root).astype(BF)
    sent = beside(root[:4], root[4:]).astype(BF)
    roots[...] = jnp.broadcast_to(sent[None], roots.shape)


def window_kernel(
    own, inner_mine, inner_other, outer_mine, outer_other, near_ids_in, near_count_in, coupling_ids_in, near_blocks,
    coupling, transfer, basis, top_transfer, top_coupling, partial, onward, shares, fifth, sixth, window, arrived, near_raw,
    near_count, coupling_raw, near_nodes, coupling_nodes, near_ids, coupling_ids, near_held, coupling_held, transfer_held, basis_held, rows_held, links_held, tall, raw_sems,
    id_sems, arrival_sems, near_sems, coupling_sems, small_sems, row_sems, link_sems, tall_sems,
):
    device = lax.axis_index("leaf") * 2 + lax.axis_index("sub")
    copy = pltpu.make_async_copy
    raw_copies = [
        copy(near_ids_in, near_raw, raw_sems.at[0]),
        copy(near_count_in, near_count, raw_sems.at[1]),
        copy(coupling_ids_in, coupling_raw, raw_sems.at[2]),
    ]
    id_copies = [copy(coupling_nodes, coupling_ids, id_sems.at[0]), copy(near_nodes, near_ids, id_sems.at[1])]
    arrivals = [
        copy(source, arrived.at[i], arrival_sems.at[i])
        for i, source in enumerate((own, inner_mine, inner_other, outer_mine, outer_other))
    ]
    small_copies = [copy(transfer, transfer_held, small_sems.at[0]), copy(basis, basis_held, small_sems.at[1])]
    places = [first + jnp.right_shift(device, t) for t, first in enumerate(FIRSTS, 1)]
    row_copies = [copy(top_transfer.at[row], rows_held.at[t], row_sems.at[t]) for t, row in enumerate(places)]
    tall_copy = copy(top_transfer.at[pl.ds(112, 14)], tall, tall_sems.at[0])
    link_copies = [copy(top_coupling.at[row], links_held.at[t], link_sems.at[t]) for t, row in enumerate(places)]
    coupling_copies = [
        copy(coupling.at[pl.ds(a, n)], coupling_held.at[pl.ds(a, n)], coupling_sems.at[i])
        for i, (a, n) in enumerate(((16, 15), (0, 16)))
    ]
    near_copies = [
        copy(near_blocks.at[pl.ds(a, 8)], near_held.at[pl.ds(a, 8)], near_sems.at[a // 8])
        for a in range(0, LEAVES, 8)
    ]
    queue = coupling_copies + near_copies
    for one in raw_copies + arrivals + queue[:1] + row_copies + link_copies + small_copies + [tall_copy] + queue[1:AHEAD]:
        one.start()

    def take(index):
        queue[index].wait()
        if index + AHEAD < len(queue):
            queue[index + AHEAD].start()

    for one in raw_copies:
        one.wait()
    near_nodes[...], coupling_nodes[...] = all_window_nodes(near_raw[...], near_count[...], coupling_raw[...])
    for one in id_copies:
        one.start()
    window[ZERO] = jnp.zeros((NV, 128), F32)
    window[ZERO + 1] = jnp.zeros((NV, 128), F32)
    for one in arrivals:
        one.wait()
    for place in range(5):
        for p in range(2 * PAIRS):
            pair = arrived[place, p].astype(F32)
            at = 2 * (place * 2 * PAIRS + p)
            window[at] = pair
            window[at + 1] = pltpu.roll(pair, K, 1)
    low = lax.broadcasted_iota(jnp.int32, (NV, 128), 1) < K

    def gathered(node, slots):
        parts = [jnp.where(low, window[node(j)], window[node(j + 1)]) for j in range(0, slots, 2)]
        return jnp.concatenate(parts, axis=1).astype(BF)

    def coupled(r):
        return dot_t(gathered(lambda j: coupling_ids[j, r], COUP), coupling_held[r])

    def near(i):
        return dot_t(gathered(lambda j: near_ids[i, j], NEAR), near_held[i])

    def descend(node, transfer_row, first):
        return dot(node.astype(BF), transfer_held[transfer_row]), beside(coupled_rows[first], coupled_rows[first + 1])

    def split(descent, added):
        top, rest = descent[:NV] + added, descent[NV:]
        return [stacked(top[:, :K], rest[:, :K]), stacked(top[:, K:], rest[:, K:])]

    def level(state, height):
        count = LEAVES >> height
        at, offset = 2 * LEAVES - 4 * count, LEAVES - 2 * count
        made = [descend(state[m], offset + m, at + 2 * m) for m in range(count)]
        return [child for one in made for child in split(*one)]

    for one in id_copies + row_copies + link_copies + small_copies + [tall_copy]:
        one.wait()
    coupled_rows = {}
    path = unit(K)
    take(0)
    for t in range(6):
        right = jnp.bitwise_and(jnp.right_shift(device, t), 1) == 1
        step = jnp.where(right, rows_held[t, :, K:], rows_held[t, :, :K])
        path = dot_t(path, step).astype(BF)
        for r in range(30 - 3 * t, max(27 - 3 * t, 15), -1):
            coupled_rows[r] = coupled(r)
        shares[:, 128 * t : 128 * t + 128] = dot(path, links_held[t]).astype(BF)
        if t < 4:
            fifth[t, :, :128] = dot(tall[8 + t, :, :K], tall[2 * t]).astype(BF)
            fifth[t, :, 128:] = dot(tall[8 + t, :, K:], tall[2 * t + 1]).astype(BF)
        else:
            sixth[t - 4, :, :256] = dot(tall[8 + t, :, :K], fifth[2 * t - 8]).astype(BF)
            sixth[t - 4, :, 256:] = dot(tall[8 + t, :, K:], fifth[2 * t - 7]).astype(BF)
    state = [stacked(coupled_rows[30], unit(K).astype(F32))]
    take(1)
    for height in (4, 3, 2):
        state = level(state, height)
        for r in range(5 * (4 - height), 5 * (4 - height) + 5):
            coupled_rows[r] = coupled(r)
    coupled_rows[15] = coupled(15)
    take(2)
    near_rows = [near(i) for i in range(2)]
    state = level(state, 1)
    near_rows += [near(i) for i in range(2, 8)]
    ends = [dot_t(state[i].astype(BF), basis_held[i]) for i in range(LEAVES)]
    take(3)
    near_rows += [near(i) for i in range(8, LEAVES)]
    for i in range(0, LEAVES, 2):
        span = slice(K * i, K * i + 128)
        pair = beside(ends[i], ends[i + 1])
        partial[:, span] = pair[:NV] + beside(near_rows[i], near_rows[i + 1])
        onward[:, span] = pair[NV:].astype(BF)


def top_kernel(roots, transfer, ids, partial, onward, shares, fifth, sixth, potential, nodes, held_ids, sems):
    device = lax.axis_index("leaf") * 2 + lax.axis_index("sub")
    id_copy = pltpu.make_async_copy(ids, held_ids, sems.at[0])
    id_copy.start()
    low4 = lax.broadcasted_iota(jnp.int32, (4, 128), 1) < K
    made = []
    for m in range(64):
        a, b = roots[2 * m].astype(F32), roots[2 * m + 1].astype(F32)
        upper = jnp.where(low4, a, pltpu.roll(b, K, 1))
        lower = jnp.where(low4, pltpu.roll(a, K, 1), b)
        made.append(dot_t(transfer[m], stacked(upper, lower).astype(BF)).astype(BF))
    for t, first in enumerate(FIRSTS):
        if 0 < t < 4:
            made = [
                dot(transfer[first + m], stacked(made[2 * m], made[2 * m + 1])).astype(BF)
                for m in range(len(made) // 2)
            ]
        elif t == 4:
            made = [dot(fifth[m], stacked(*third[4 * m : 4 * m + 4])).astype(BF) for m in range(4)]
        elif t == 5:
            made = [dot(sixth[m], stacked(*third[8 * m : 8 * m + 8])).astype(BF) for m in range(2)]
        if t == 2:
            third = made
        for m, node in enumerate(made):
            nodes[first + m] = node
    id_copy.wait()
    sources = []
    for t, first in enumerate(FIRSTS, 1):
        row = first + jnp.right_shift(device, t)
        sources += [nodes[first + held_ids[0, row]], nodes[first + held_ids[1, row]]]
    incoming = dot(shares[...], stacked(*sources)).T.astype(BF)
    potential[...] = partial[...] + dot(incoming, onward[...])


def spec(space):
    return pl.BlockSpec(memory_space=space)


VMEM, SMEM, ANY = pltpu.VMEM, pltpu.SMEM, pl.ANY


def exchanged(core, pairs):
    return [(2 * a + core, 2 * b + core) for c, d in pairs for a, b in ((c, d), (d, c))]


INNER = exchanged(0, [(c, c + 1) for c in range(0, 64, 2)]) + exchanged(
    1, [(c, c + 2) for c in range(64) if c % 4 < 2]
)
OUTER = (
    exchanged(0, [(c, c + 1) for c in range(1, 63, 2)])
    + exchanged(1, [(c, c + 2) for c in range(62) if c % 4 >= 2])
    + [(0, 1), (1, 3), (3, 0), (126, 127), (127, 125), (125, 126)]
)


def local(
    density, basis, near_ids, near_count, near_blocks, local_transfer, local_coupling, local_coupling_ids,
    top_transfer, top_coupling, top_coupling_ids,
):
    shape = jax.ShapeDtypeStruct
    pack, roots = pl.pallas_call(
        upward_kernel,
        out_shape=(shape((PAIRS, NV, 128), BF), shape((128, 4, 128), BF)),
        in_specs=[spec(VMEM)] * 3,
        out_specs=(spec(VMEM),) * 2,
        cost_estimate=pl.CostEstimate(flops=20_000_000_000, bytes_accessed=1_000_000, transcendentals=0),
        compiler_params=pltpu.CompilerParams(vmem_limit_bytes=56 << 20),
        name="upward",
    )(density, basis, local_transfer)
    every = ("leaf", "sub")
    own = jnp.concatenate([pack, lax.ppermute(pack, "sub", [(0, 1), (1, 0)])])
    inner_mine = lax.ppermute(own, every, INNER)
    outer_mine = lax.ppermute(own, every, OUTER)
    all_roots = lax.all_to_all(roots, every, 0, 0, tiled=True)
    inner_other = lax.ppermute(inner_mine, "sub", [(0, 1), (1, 0)])
    outer_other = lax.ppermute(outer_mine, "sub", [(0, 1), (1, 0)])
    partial, onward, shares, fifth, sixth = pl.pallas_call(
        window_kernel,
        out_shape=(
            shape((NV, 1024), F32),
            shape((K, 1024), BF),
            shape((K, 768), BF),
            shape((4, K, 256), BF),
            shape((2, K, 512), BF),
        ),
        in_specs=[spec(ANY)] * 14,
        out_specs=(spec(VMEM),) * 5,
        scratch_shapes=[
            pltpu.VMEM((ZERO + 2, NV, 128), F32),
            pltpu.VMEM((5, 2 * PAIRS, NV, 128), BF),
            pltpu.VMEM((LEAVES, NEAR), jnp.int32),
            pltpu.VMEM((1, LEAVES), jnp.int32),
            pltpu.VMEM((COUP, 2 * LEAVES - 1), jnp.int32),
            pltpu.VMEM((LEAVES, NEAR), jnp.int32),
            pltpu.VMEM((COUP, 2 * LEAVES - 1), jnp.int32),
            pltpu.SMEM((LEAVES, NEAR), jnp.int32),
            pltpu.SMEM((COUP, 2 * LEAVES - 1), jnp.int32),
            pltpu.VMEM((LEAVES, 64, NEAR * 64), BF),
            pltpu.VMEM((2 * LEAVES - 1, K, COUP * K), BF),
            pltpu.VMEM((LEAVES - 1, K, 128), BF),
            pltpu.VMEM((LEAVES, 64, K), BF),
            pltpu.VMEM((6, K, 128), BF),
            pltpu.VMEM((6, K, 128), BF),
            pltpu.VMEM((14, K, 128), BF),
            pltpu.SemaphoreType.DMA((3,)),
            pltpu.SemaphoreType.DMA((2,)),
            pltpu.SemaphoreType.DMA((5,)),
            pltpu.SemaphoreType.DMA((4,)),
            pltpu.SemaphoreType.DMA((3,)),
            pltpu.SemaphoreType.DMA((2,)),
            pltpu.SemaphoreType.DMA((6,)),
            pltpu.SemaphoreType.DMA((6,)),
            pltpu.SemaphoreType.DMA((1,)),
        ],
        compiler_params=pltpu.CompilerParams(vmem_limit_bytes=52 << 20),
        cost_estimate=pl.CostEstimate(flops=120_000_000, bytes_accessed=8_000_000, transcendentals=0),
        name="window",
    )(
        own, inner_mine, inner_other, outer_mine, outer_other, near_ids, near_count.reshape(1, LEAVES),
        local_coupling_ids.T, near_blocks, local_coupling, local_transfer, basis, top_transfer, top_coupling,
    )
    return pl.pallas_call(
        top_kernel,
        out_shape=shape((NV, 1024), F32),
        in_specs=[spec(VMEM)] * 2 + [spec(ANY)] + [spec(VMEM)] * 5,
        out_specs=spec(VMEM),
        scratch_shapes=[
            pltpu.VMEM((TOP, K, NV), BF),
            pltpu.SMEM((2, TOP), jnp.int32),
            pltpu.SemaphoreType.DMA((1,)),
        ],
        compiler_params=pltpu.CompilerParams(vmem_limit_bytes=20 << 20),
        name="top",
    )(all_roots, top_transfer, top_coupling_ids.T, partial, onward, shares, fifth, sixth)


def solution(mesh):
    in_specs = (
        P(None, ("leaf", "sub")),
        P(("leaf", "sub"), None, None),
        P(("leaf", "sub"), None),
        P(("leaf", "sub")),
        P(("leaf", "sub"), None, None),
        P(("leaf", "sub"), None, None),
        P(("leaf", "sub"), None, None),
        P(("leaf", "sub"), None),
        P(),
        P(),
        P(),
    )
    out_specs = P(None, ("leaf", "sub"))
    return jax.shard_map(local, mesh=mesh, in_specs=in_specs, out_specs=out_specs, check_vma=False)
```

```python
import jax
import jax.numpy as jnp
from jax import lax
from jax.experimental import pallas as pl
from jax.experimental.pallas import tpu as pltpu
from jax.sharding import PartitionSpec as P

NV = 8
K = 64
LEAVES = 16
NEAR = 24
COUP = 16
HEIGHTS = 5
PAIRS = 24
NODES = 2 * PAIRS
LEVEL_OFFSETS = (16, 32, 40, 44, 46)
ZERO = 5 * 2 * NODES
TOP = 126
AHEAD = 3
FIRSTS = (0, 64, 96, 112, 120, 124)
BF = jnp.bfloat16
F32 = jnp.float32


def dot(a, b):
    return lax.dot_general(a, b, (((1,), (0,)), ((), ())), preferred_element_type=F32)


def dot_t(a, b):
    return lax.dot_general(a, b, (((1,), (1,)), ((), ())), preferred_element_type=F32)


def unit(n):
    return (lax.broadcasted_iota(jnp.int32, (n, n), 0) == lax.broadcasted_iota(jnp.int32, (n, n), 1)).astype(BF)


def stacked(*parts):
    return jnp.concatenate(parts, axis=0)


def turned(columns):
    high = columns.astype(BF)
    rest = (columns - high.astype(F32)).astype(BF)
    return dot_t(unit(NV), high) + dot_t(unit(NV), rest)


def beside(a, b):
    return jnp.concatenate([a, b], axis=1)


def window_nodes(ids, height, offset, leaf, sub, live, slot_axis):
    shift = jnp.broadcast_to(4 - height, ids.shape)
    slot = jnp.right_shift(ids, shift)
    node = ids - jnp.left_shift(slot, shift)
    delta = jnp.right_shift(slot, 1) - 2
    core = jnp.bitwise_and(slot, 1)
    chip = leaf + delta
    odd, upper = jnp.bitwise_and(leaf, 1), jnp.bitwise_and(jnp.right_shift(leaf, 1), 1)
    place = jnp.where(delta == 1 - 2 * odd, 1 + sub, jnp.where(delta == 2 * odd - 1, 3 + sub, 0))
    place = jnp.where(delta == 2 - 4 * upper, 2 - sub, jnp.where(delta == 4 * upper - 2, 4 - sub, place))
    second = core ^ sub ^ ((place == 2) | (place == 4)).astype(jnp.int32)
    index = (place * 2 + second) * NODES + offset + node
    live = live & (chip >= 0) & (chip < 64)
    index = jnp.where(live, index, ZERO)
    column = lax.broadcasted_iota(jnp.int32, ids.shape, slot_axis)
    return index ^ jnp.bitwise_and(column, 1)


def all_window_nodes(near_ids, near_count, coupling_ids):
    leaf, sub = lax.axis_index("leaf"), lax.axis_index("sub")
    slots = lax.broadcasted_iota(jnp.int32, near_ids.shape, 1)
    diagonal = lax.broadcasted_iota(jnp.int32, (LEAVES, LEAVES), 0) == lax.broadcasted_iota(
        jnp.int32, (LEAVES, LEAVES), 1
    )
    counts = jnp.sum(jnp.where(diagonal, near_count, 0), axis=1, keepdims=True)
    near_nodes = window_nodes(near_ids, 0, 0, leaf, sub, slots < counts, 1)
    rows = lax.broadcasted_iota(jnp.int32, coupling_ids.shape, 1)
    height = sum((rows >= 2 * LEAVES - 2 * (LEAVES >> h)).astype(jnp.int32) for h in range(1, HEIGHTS))
    offset = jnp.zeros(coupling_ids.shape, jnp.int32)
    for h, place in enumerate(LEVEL_OFFSETS):
        offset = jnp.where(height == h, place, offset)
    coupling_nodes = window_nodes(coupling_ids, height, offset, leaf, sub, coupling_ids >= 0, 0)
    return near_nodes, coupling_nodes


def upward_kernel(density, basis, transfer, pack, roots):
    level = []
    block = lax.broadcasted_iota(jnp.int32, (4 * NV, 256), 0) // NV
    own_lanes = block == lax.broadcasted_iota(jnp.int32, (4 * NV, 256), 1) // K
    for q in range(4):
        four = density[:, 256 * q : 256 * q + 256]
        pack[2 * q], pack[2 * q + 1] = four[:, :128], four[:, 128:]
        four = four.astype(F32)
        spread = jnp.where(own_lanes, stacked(four, four, four, four), 0.0).astype(BF)
        made = dot(spread, basis[4 * q : 4 * q + 4].reshape(256, K))
        for half in range(2):
            at = 16 * half
            joined = beside(made[at : at + NV], made[at + NV : at + 16]).astype(BF)
            pack[8 + 2 * q + half] = joined
            level.append(joined)
    grand = [
        beside(
            dot(transfer[8 + q, :, :K], transfer[2 * q]).astype(BF),
            dot(transfer[8 + q, :, K:], transfer[2 * q + 1]).astype(BF),
        )
        for q in range(4)
    ]
    root_map = beside(
        dot(transfer[14, :, :K], transfer[12]).astype(BF), dot(transfer[14, :, K:], transfer[13]).astype(BF)
    )
    second = [dot_t(grand[q], beside(level[2 * q], level[2 * q + 1])).astype(BF) for q in range(4)]
    first = [dot_t(transfer[m], pair).astype(BF) for m, pair in enumerate(level)]
    top = dot(root_map, stacked(*second)).astype(BF)
    third = [dot(transfer[12 + q], stacked(second[2 * q], second[2 * q + 1])).astype(BF) for q in range(2)]
    rows = stacked(*first, *second, *third, top).astype(F32).T
    for q in range(7):
        pack[16 + q] = rows[:, 128 * q : 128 * q + 128].astype(BF)
    root = rows[:, 896:]
    pack[23] = beside(root, root).astype(BF)
    sent = beside(root[:4], root[4:]).astype(BF)
    roots[...] = jnp.broadcast_to(sent[None], roots.shape)


def window_kernel(
    own, inner_mine, inner_other, outer_mine, outer_other, near_ids_in, near_count_in, coupling_ids_in, near_blocks,
    coupling, transfer, basis, top_transfer, top_coupling, partial, onward, shares, fifth, sixth, window, arrived, near_raw,
    near_count, coupling_raw, near_nodes, coupling_nodes, near_ids, coupling_ids, near_held, coupling_held, transfer_held, basis_held, rows_held, links_held, tall, raw_sems,
    id_sems, arrival_sems, near_sems, coupling_sems, small_sems, row_sems, link_sems, tall_sems,
):
    device = lax.axis_index("leaf") * 2 + lax.axis_index("sub")
    copy = pltpu.make_async_copy
    raw_copies = [
        copy(near_ids_in, near_raw, raw_sems.at[0]),
        copy(near_count_in, near_count, raw_sems.at[1]),
        copy(coupling_ids_in, coupling_raw, raw_sems.at[2]),
    ]
    id_copies = [copy(coupling_nodes, coupling_ids, id_sems.at[0]), copy(near_nodes, near_ids, id_sems.at[1])]
    arrivals = [
        copy(source, arrived.at[i], arrival_sems.at[i])
        for i, source in enumerate((own, inner_mine, inner_other, outer_mine, outer_other))
    ]
    small_copies = [copy(transfer, transfer_held, small_sems.at[0]), copy(basis, basis_held, small_sems.at[1])]
    places = [first + jnp.right_shift(device, t) for t, first in enumerate(FIRSTS, 1)]
    row_copies = [copy(top_transfer.at[row], rows_held.at[t], row_sems.at[t]) for t, row in enumerate(places)]
    tall_copy = copy(top_transfer.at[pl.ds(112, 14)], tall, tall_sems.at[0])
    link_copies = [copy(top_coupling.at[row], links_held.at[t], link_sems.at[t]) for t, row in enumerate(places)]
    coupling_copies = [
        copy(coupling.at[pl.ds(a, n)], coupling_held.at[pl.ds(a, n)], coupling_sems.at[i])
        for i, (a, n) in enumerate(((16, 15), (0, 16)))
    ]
    near_copies = [
        copy(near_blocks.at[pl.ds(a, 8)], near_held.at[pl.ds(a, 8)], near_sems.at[a // 8])
        for a in range(0, LEAVES, 8)
    ]
    queue = coupling_copies + near_copies
    for one in raw_copies + arrivals + queue[:1] + row_copies + link_copies + small_copies + [tall_copy] + queue[1:AHEAD]:
        one.start()

    def take(index):
        queue[index].wait()
        if index + AHEAD < len(queue):
            queue[index + AHEAD].start()

    for one in raw_copies:
        one.wait()
    near_nodes[...], coupling_nodes[...] = all_window_nodes(near_raw[...], near_count[...], coupling_raw[...])
    for one in id_copies:
        one.start()
    window[ZERO] = jnp.zeros((NV, 128), F32)
    window[ZERO + 1] = jnp.zeros((NV, 128), F32)
    for one in arrivals:
        one.wait()
    for place in range(5):
        for p in range(2 * PAIRS):
            pair = arrived[place, p].astype(F32)
            at = 2 * (place * 2 * PAIRS + p)
            window[at] = pair
            window[at + 1] = pltpu.roll(pair, K, 1)
    low = lax.broadcasted_iota(jnp.int32, (NV, 128), 1) < K

    def gathered(node, slots):
        parts = [jnp.where(low, window[node(j)], window[node(j + 1)]) for j in range(0, slots, 2)]
        return jnp.concatenate(parts, axis=1).astype(BF)

    def coupled(r):
        return dot_t(gathered(lambda j: coupling_ids[j, r], COUP), coupling_held[r])

    def near(i):
        return dot_t(gathered(lambda j: near_ids[i, j], NEAR), near_held[i])

    def descend(node, transfer_row, first):
        return dot(node.astype(BF), transfer_held[transfer_row]), beside(coupled_rows[first], coupled_rows[first + 1])

    def split(descent, added):
        top, rest = descent[:NV] + added, descent[NV:]
        return [stacked(top[:, :K], rest[:, :K]), stacked(top[:, K:], rest[:, K:])]

    def level(state, height):
        count = LEAVES >> height
        at, offset = 2 * LEAVES - 4 * count, LEAVES - 2 * count
        made = [descend(state[m], offset + m, at + 2 * m) for m in range(count)]
        return [child for one in made for child in split(*one)]

    for one in id_copies + row_copies + link_copies + small_copies + [tall_copy]:
        one.wait()
    coupled_rows = {}
    path = unit(K)
    take(0)
    for t in range(6):
        right = jnp.bitwise_and(jnp.right_shift(device, t), 1) == 1
        step = jnp.where(right, rows_held[t, :, K:], rows_held[t, :, :K])
        path = dot_t(path, step).astype(BF)
        for r in range(30 - 3 * t, max(27 - 3 * t, 15), -1):
            coupled_rows[r] = coupled(r)
        shares[:, 128 * t : 128 * t + 128] = dot(path, links_held[t]).astype(BF)
        if t < 4:
            fifth[t, :, :128] = dot(tall[8 + t, :, :K], tall[2 * t]).astype(BF)
            fifth[t, :, 128:] = dot(tall[8 + t, :, K:], tall[2 * t + 1]).astype(BF)
        else:
            sixth[t - 4, :, :256] = dot(tall[8 + t, :, :K], fifth[2 * t - 8]).astype(BF)
            sixth[t - 4, :, 256:] = dot(tall[8 + t, :, K:], fifth[2 * t - 7]).astype(BF)
    state = [stacked(coupled_rows[30], unit(K).astype(F32))]
    take(1)
    for height in (4, 3, 2):
        state = level(state, height)
        for r in range(5 * (4 - height), 5 * (4 - height) + 5):
            coupled_rows[r] = coupled(r)
    coupled_rows[15] = coupled(15)
    take(2)
    near_rows = [near(i) for i in range(2)]
    state = level(state, 1)
    near_rows += [near(i) for i in range(2, 8)]
    ends = [dot_t(state[i].astype(BF), basis_held[i]) for i in range(LEAVES)]
    take(3)
    near_rows += [near(i) for i in range(8, LEAVES)]
    for i in range(0, LEAVES, 2):
        span = slice(K * i, K * i + 128)
        pair = beside(ends[i], ends[i + 1])
        partial[:, span] = pair[:NV] + beside(near_rows[i], near_rows[i + 1])
        onward[:, span] = pair[NV:].astype(BF)


def top_kernel(roots, transfer, ids, partial, onward, shares, fifth, sixth, potential, nodes, held_ids, sems):
    device = lax.axis_index("leaf") * 2 + lax.axis_index("sub")
    id_copy = pltpu.make_async_copy(ids, held_ids, sems.at[0])
    id_copy.start()
    low4 = lax.broadcasted_iota(jnp.int32, (4, 128), 1) < K

    def pair(m):
        a, b = roots[2 * m].astype(F32), roots[2 * m + 1].astype(F32)
        upper = jnp.where(low4, a, pltpu.roll(b, K, 1))
        lower = jnp.where(low4, pltpu.roll(a, K, 1), b)
        return stacked(upper, lower)

    side = lax.broadcasted_iota(jnp.int32, (128, 2 * NV), 1) // NV
    blank, none = jnp.zeros((NV, 128), F32), jnp.zeros((128, 2 * NV), BF)
    made = []
    for m in range(32):
        rows = stacked(beside(pair(m), blank), beside(blank, pair(m + 32))).astype(BF)
        made.append(dot_t(beside(transfer[m], transfer[m + 32]), rows).astype(BF))
    for t, first in enumerate(FIRSTS):
        half = 32 >> t
        if 0 < t < 4:
            below, made = made, []
            for m in range(half):
                both = stacked(below[2 * m], below[2 * m + 1])
                both = stacked(jnp.where(side == 0, both, none), jnp.where(side == 1, both, none))
                made.append(dot(beside(transfer[first + m], transfer[first + half + m]), both).astype(BF))
        elif t >= 4:
            maps, span = (fifth, 4) if t == 4 else (sixth, 8)
            below, made = third, []
            for m in range(half):
                both = stacked(*below[span * m : span * m + span])
                ends = dot(maps[m], both), dot(maps[half + m], both)
                made.append(jnp.where(side[:K] == 0, *ends).astype(BF))
        if t == 2:
            third = made
        for m, node in enumerate(made):
            nodes[first + m] = node
    id_copy.wait()
    sources = []
    for t, first in enumerate(FIRSTS, 1):
        row, half = first + jnp.right_shift(device, t), 64 >> t
        for end in range(2):
            node = held_ids[end, row]
            upper_half = (node >= half).astype(jnp.int32)
            found = nodes[first + jnp.bitwise_and(node, half - 1)]
            sources.append(jnp.where(side[:K] == upper_half, found, none[:K]))
    incoming = dot(shares[...], stacked(*sources)).T
    incoming = (incoming[:NV] + incoming[NV:]).astype(BF)
    potential[...] = partial[...] + dot(incoming, onward[...])


def spec(space):
    return pl.BlockSpec(memory_space=space)


VMEM, SMEM, ANY = pltpu.VMEM, pltpu.SMEM, pl.ANY


def exchanged(core, pairs):
    return [(2 * a + core, 2 * b + core) for c, d in pairs for a, b in ((c, d), (d, c))]


INNER = exchanged(0, [(c, c + 1) for c in range(0, 64, 2)]) + exchanged(
    1, [(c, c + 2) for c in range(64) if c % 4 < 2]
)
OUTER = (
    exchanged(0, [(c, c + 1) for c in range(1, 63, 2)])
    + exchanged(1, [(c, c + 2) for c in range(62) if c % 4 >= 2])
    + [(0, 1), (1, 3), (3, 0), (126, 127), (127, 125), (125, 126)]
)


def local(
    density, basis, near_ids, near_count, near_blocks, local_transfer, local_coupling, local_coupling_ids,
    top_transfer, top_coupling, top_coupling_ids,
):
    shape = jax.ShapeDtypeStruct
    pack, roots = pl.pallas_call(
        upward_kernel,
        out_shape=(shape((PAIRS, NV, 128), BF), shape((128, 4, 128), BF)),
        in_specs=[spec(VMEM)] * 3,
        out_specs=(spec(VMEM),) * 2,
        cost_estimate=pl.CostEstimate(flops=20_000_000_000, bytes_accessed=1_000_000, transcendentals=0),
        compiler_params=pltpu.CompilerParams(vmem_limit_bytes=56 << 20),
        name="upward",
    )(density, basis, local_transfer)
    every = ("leaf", "sub")
    own = jnp.concatenate([pack, lax.ppermute(pack, "sub", [(0, 1), (1, 0)])])
    inner_mine = lax.ppermute(own, every, INNER)
    outer_mine = lax.ppermute(own, every, OUTER)
    all_roots = lax.all_to_all(roots, every, 0, 0, tiled=True)
    inner_other = lax.ppermute(inner_mine, "sub", [(0, 1), (1, 0)])
    outer_other = lax.ppermute(outer_mine, "sub", [(0, 1), (1, 0)])
    partial, onward, shares, fifth, sixth = pl.pallas_call(
        window_kernel,
        out_shape=(
            shape((NV, 1024), F32),
            shape((K, 1024), BF),
            shape((K, 768), BF),
            shape((4, K, 256), BF),
            shape((2, K, 512), BF),
        ),
        in_specs=[spec(ANY)] * 14,
        out_specs=(spec(VMEM),) * 5,
        scratch_shapes=[
            pltpu.VMEM((ZERO + 2, NV, 128), F32),
            pltpu.VMEM((5, 2 * PAIRS, NV, 128), BF),
            pltpu.VMEM((LEAVES, NEAR), jnp.int32),
            pltpu.VMEM((1, LEAVES), jnp.int32),
            pltpu.VMEM((COUP, 2 * LEAVES - 1), jnp.int32),
            pltpu.VMEM((LEAVES, NEAR), jnp.int32),
            pltpu.VMEM((COUP, 2 * LEAVES - 1), jnp.int32),
            pltpu.SMEM((LEAVES, NEAR), jnp.int32),
            pltpu.SMEM((COUP, 2 * LEAVES - 1), jnp.int32),
            pltpu.VMEM((LEAVES, 64, NEAR * 64), BF),
            pltpu.VMEM((2 * LEAVES - 1, K, COUP * K), BF),
            pltpu.VMEM((LEAVES - 1, K, 128), BF),
            pltpu.VMEM((LEAVES, 64, K), BF),
            pltpu.VMEM((6, K, 128), BF),
            pltpu.VMEM((6, K, 128), BF),
            pltpu.VMEM((14, K, 128), BF),
            pltpu.SemaphoreType.DMA((3,)),
            pltpu.SemaphoreType.DMA((2,)),
            pltpu.SemaphoreType.DMA((5,)),
            pltpu.SemaphoreType.DMA((4,)),
            pltpu.SemaphoreType.DMA((3,)),
            pltpu.SemaphoreType.DMA((2,)),
            pltpu.SemaphoreType.DMA((6,)),
            pltpu.SemaphoreType.DMA((6,)),
            pltpu.SemaphoreType.DMA((1,)),
        ],
        compiler_params=pltpu.CompilerParams(vmem_limit_bytes=52 << 20),
        cost_estimate=pl.CostEstimate(flops=120_000_000, bytes_accessed=8_000_000, transcendentals=0),
        name="window",
    )(
        own, inner_mine, inner_other, outer_mine, outer_other, near_ids, near_count.reshape(1, LEAVES),
        local_coupling_ids.T, near_blocks, local_coupling, local_transfer, basis, top_transfer, top_coupling,
    )
    return pl.pallas_call(
        top_kernel,
        out_shape=shape((NV, 1024), F32),
        in_specs=[spec(VMEM)] * 2 + [spec(ANY)] + [spec(VMEM)] * 5,
        out_specs=spec(VMEM),
        scratch_shapes=[
            pltpu.VMEM((TOP, K, 2 * NV), BF),
            pltpu.SMEM((2, TOP), jnp.int32),
            pltpu.SemaphoreType.DMA((1,)),
        ],
        compiler_params=pltpu.CompilerParams(vmem_limit_bytes=20 << 20),
        name="top",
    )(all_roots, top_transfer, top_coupling_ids.T, partial, onward, shares, fifth, sixth)


def solution(mesh):
    in_specs = (
        P(None, ("leaf", "sub")),
        P(("leaf", "sub"), None, None),
        P(("leaf", "sub"), None),
        P(("leaf", "sub")),
        P(("leaf", "sub"), None, None),
        P(("leaf", "sub"), None, None),
        P(("leaf", "sub"), None, None),
        P(("leaf", "sub"), None),
        P(),
        P(),
        P(),
    )
    out_specs = P(None, ("leaf", "sub"))
    return jax.shard_map(local, mesh=mesh, in_specs=in_specs, out_specs=out_specs, check_vma=False)
```

```python
import jax
import jax.numpy as jnp
from jax import lax
from jax.experimental import pallas as pl
from jax.experimental.pallas import tpu as pltpu
from jax.sharding import PartitionSpec as P

NV = 8
K = 64
LEAVES = 16
NEAR = 24
COUP = 16
HEIGHTS = 5
PAIRS = 24
NODES = 2 * PAIRS
LEVEL_OFFSETS = (16, 32, 40, 44, 46)
ZERO = 5 * 2 * NODES
TOP = 126
AHEAD = 3
FIRSTS = (0, 64, 96, 112, 120, 124)
BF = jnp.bfloat16
F32 = jnp.float32


def dot(a, b):
    return lax.dot_general(a, b, (((1,), (0,)), ((), ())), preferred_element_type=F32)


def dot_t(a, b):
    return lax.dot_general(a, b, (((1,), (1,)), ((), ())), preferred_element_type=F32)


def unit(n):
    return (lax.broadcasted_iota(jnp.int32, (n, n), 0) == lax.broadcasted_iota(jnp.int32, (n, n), 1)).astype(BF)


def stacked(*parts):
    return jnp.concatenate(parts, axis=0)


def turned(columns):
    high = columns.astype(BF)
    rest = (columns - high.astype(F32)).astype(BF)
    return dot_t(unit(NV), high) + dot_t(unit(NV), rest)


def beside(a, b):
    return jnp.concatenate([a, b], axis=1)


def window_nodes(ids, height, offset, leaf, sub, live, slot_axis):
    shift = jnp.broadcast_to(4 - height, ids.shape)
    slot = jnp.right_shift(ids, shift)
    node = ids - jnp.left_shift(slot, shift)
    delta = jnp.right_shift(slot, 1) - 2
    core = jnp.bitwise_and(slot, 1)
    chip = leaf + delta
    odd, upper = jnp.bitwise_and(leaf, 1), jnp.bitwise_and(jnp.right_shift(leaf, 1), 1)
    place = jnp.where(delta == 1 - 2 * odd, 1 + sub, jnp.where(delta == 2 * odd - 1, 3 + sub, 0))
    place = jnp.where(delta == 2 - 4 * upper, 2 - sub, jnp.where(delta == 4 * upper - 2, 4 - sub, place))
    second = core ^ sub ^ ((place == 2) | (place == 4)).astype(jnp.int32)
    index = (place * 2 + second) * NODES + offset + node
    live = live & (chip >= 0) & (chip < 64)
    index = jnp.where(live, index, ZERO)
    column = lax.broadcasted_iota(jnp.int32, ids.shape, slot_axis)
    return index ^ jnp.bitwise_and(column, 1)


def all_window_nodes(near_ids, near_count, coupling_ids):
    leaf, sub = lax.axis_index("leaf"), lax.axis_index("sub")
    slots = lax.broadcasted_iota(jnp.int32, near_ids.shape, 1)
    diagonal = lax.broadcasted_iota(jnp.int32, (LEAVES, LEAVES), 0) == lax.broadcasted_iota(
        jnp.int32, (LEAVES, LEAVES), 1
    )
    counts = jnp.sum(jnp.where(diagonal, near_count, 0), axis=1, keepdims=True)
    near_nodes = window_nodes(near_ids, 0, 0, leaf, sub, slots < counts, 1)
    rows = lax.broadcasted_iota(jnp.int32, coupling_ids.shape, 1)
    height = sum((rows >= 2 * LEAVES - 2 * (LEAVES >> h)).astype(jnp.int32) for h in range(1, HEIGHTS))
    offset = jnp.zeros(coupling_ids.shape, jnp.int32)
    for h, place in enumerate(LEVEL_OFFSETS):
        offset = jnp.where(height == h, place, offset)
    coupling_nodes = window_nodes(coupling_ids, height, offset, leaf, sub, coupling_ids >= 0, 0)
    return near_nodes, coupling_nodes


def upward_kernel(density, basis, transfer, pack, roots):
    level = []
    block = lax.broadcasted_iota(jnp.int32, (4 * NV, 256), 0) // NV
    own_lanes = block == lax.broadcasted_iota(jnp.int32, (4 * NV, 256), 1) // K
    for q in range(4):
        four = density[:, 256 * q : 256 * q + 256]
        pack[2 * q], pack[2 * q + 1] = four[:, :128], four[:, 128:]
        four = four.astype(F32)
        spread = jnp.where(own_lanes, stacked(four, four, four, four), 0.0).astype(BF)
        made = dot(spread, basis[4 * q : 4 * q + 4].reshape(256, K))
        for half in range(2):
            at = 16 * half
            joined = beside(made[at : at + NV], made[at + NV : at + 16]).astype(BF)
            pack[8 + 2 * q + half] = joined
            level.append(joined)
    grand = [
        beside(
            dot(transfer[8 + q, :, :K], transfer[2 * q]).astype(BF),
            dot(transfer[8 + q, :, K:], transfer[2 * q + 1]).astype(BF),
        )
        for q in range(4)
    ]
    root_map = beside(
        dot(transfer[14, :, :K], transfer[12]).astype(BF), dot(transfer[14, :, K:], transfer[13]).astype(BF)
    )
    second = [dot_t(grand[q], beside(level[2 * q], level[2 * q + 1])).astype(BF) for q in range(4)]
    first = [dot_t(transfer[m], pair).astype(BF) for m, pair in enumerate(level)]
    top = dot(root_map, stacked(*second)).astype(BF)
    third = [dot(transfer[12 + q], stacked(second[2 * q], second[2 * q + 1])).astype(BF) for q in range(2)]
    lower = stacked(*first, *second).astype(F32).T
    rows = stacked(*third, top).astype(F32).T
    for q in range(6):
        pack[16 + q] = lower[:, 128 * q : 128 * q + 128].astype(BF)
    pack[22] = rows[:, :128].astype(BF)
    root = rows[:, 128:]
    pack[23] = beside(root, root).astype(BF)
    sent = beside(root[:4], root[4:]).astype(BF)
    roots[...] = jnp.broadcast_to(sent[None], roots.shape)


def window_kernel(
    own, inner_mine, inner_other, outer_mine, outer_other, near_ids_in, near_count_in, coupling_ids_in, near_blocks,
    coupling, transfer, basis, top_transfer, top_coupling, partial, onward, shares, fifth, sixth, window, arrived, near_raw,
    near_count, coupling_raw, near_nodes, coupling_nodes, near_ids, coupling_ids, near_held, coupling_held, transfer_held, basis_held, rows_held, links_held, tall, raw_sems,
    id_sems, arrival_sems, near_sems, coupling_sems, small_sems, row_sems, link_sems, tall_sems,
):
    device = lax.axis_index("leaf") * 2 + lax.axis_index("sub")
    copy = pltpu.make_async_copy
    raw_copies = [
        copy(near_ids_in, near_raw, raw_sems.at[0]),
        copy(near_count_in, near_count, raw_sems.at[1]),
        copy(coupling_ids_in, coupling_raw, raw_sems.at[2]),
    ]
    id_copies = [copy(coupling_nodes, coupling_ids, id_sems.at[0]), copy(near_nodes, near_ids, id_sems.at[1])]
    arrivals = [
        copy(source, arrived.at[i], arrival_sems.at[i])
        for i, source in enumerate((own, inner_mine, inner_other, outer_mine, outer_other))
    ]
    small_copies = [copy(transfer, transfer_held, small_sems.at[0]), copy(basis, basis_held, small_sems.at[1])]
    places = [first + jnp.right_shift(device, t) for t, first in enumerate(FIRSTS, 1)]
    row_copies = [copy(top_transfer.at[row], rows_held.at[t], row_sems.at[t]) for t, row in enumerate(places)]
    tall_copy = copy(top_transfer.at[pl.ds(112, 14)], tall, tall_sems.at[0])
    link_copies = [copy(top_coupling.at[row], links_held.at[t], link_sems.at[t]) for t, row in enumerate(places)]
    coupling_copies = [
        copy(coupling.at[pl.ds(a, n)], coupling_held.at[pl.ds(a, n)], coupling_sems.at[i])
        for i, (a, n) in enumerate(((16, 15), (0, 16)))
    ]
    near_copies = [
        copy(near_blocks.at[pl.ds(a, 8)], near_held.at[pl.ds(a, 8)], near_sems.at[a // 8])
        for a in range(0, LEAVES, 8)
    ]
    queue = coupling_copies + near_copies
    for one in raw_copies + arrivals + queue[:1] + row_copies + link_copies + small_copies + [tall_copy] + queue[1:AHEAD]:
        one.start()

    def take(index):
        queue[index].wait()
        if index + AHEAD < len(queue):
            queue[index + AHEAD].start()

    for one in raw_copies:
        one.wait()
    near_nodes[...], coupling_nodes[...] = all_window_nodes(near_raw[...], near_count[...], coupling_raw[...])
    for one in id_copies:
        one.start()
    window[ZERO] = jnp.zeros((NV, 128), F32)
    window[ZERO + 1] = jnp.zeros((NV, 128), F32)
    for one in arrivals:
        one.wait()
    for place in range(5):
        for p in range(2 * PAIRS):
            pair = arrived[place, p].astype(F32)
            at = 2 * (place * 2 * PAIRS + p)
            window[at] = pair
            window[at + 1] = pltpu.roll(pair, K, 1)
    low = lax.broadcasted_iota(jnp.int32, (NV, 128), 1) < K

    def gathered(node, slots):
        parts = [jnp.where(low, window[node(j)], window[node(j + 1)]) for j in range(0, slots, 2)]
        return jnp.concatenate(parts, axis=1).astype(BF)

    def coupled(r):
        return dot_t(gathered(lambda j: coupling_ids[j, r], COUP), coupling_held[r])

    def near(i):
        return dot_t(gathered(lambda j: near_ids[i, j], NEAR), near_held[i])

    def descend(node, transfer_row, first):
        return dot(node.astype(BF), transfer_held[transfer_row]), beside(coupled_rows[first], coupled_rows[first + 1])

    def split(descent, added):
        top, rest = descent[:NV] + added, descent[NV:]
        return [stacked(top[:, :K], rest[:, :K]), stacked(top[:, K:], rest[:, K:])]

    def level(state, height):
        count = LEAVES >> height
        at, offset = 2 * LEAVES - 4 * count, LEAVES - 2 * count
        made = [descend(state[m], offset + m, at + 2 * m) for m in range(count)]
        return [child for one in made for child in split(*one)]

    for one in id_copies + row_copies + link_copies + small_copies + [tall_copy]:
        one.wait()
    coupled_rows = {}
    path = unit(K)
    take(0)
    for t in range(6):
        right = jnp.bitwise_and(jnp.right_shift(device, t), 1) == 1
        step = jnp.where(right, rows_held[t, :, K:], rows_held[t, :, :K])
        path = dot_t(path, step).astype(BF)
        for r in range(30 - 3 * t, max(27 - 3 * t, 15), -1):
            coupled_rows[r] = coupled(r)
        shares[:, 128 * t : 128 * t + 128] = dot(path, links_held[t]).astype(BF)
        if t < 4:
            fifth[t, :, :128] = dot(tall[8 + t, :, :K], tall[2 * t]).astype(BF)
            fifth[t, :, 128:] = dot(tall[8 + t, :, K:], tall[2 * t + 1]).astype(BF)
        else:
            sixth[t - 4, :, :256] = dot(tall[8 + t, :, :K], fifth[2 * t - 8]).astype(BF)
            sixth[t - 4, :, 256:] = dot(tall[8 + t, :, K:], fifth[2 * t - 7]).astype(BF)
    state = [stacked(coupled_rows[30], unit(K).astype(F32))]
    take(1)
    for height in (4, 3, 2):
        state = level(state, height)
        for r in range(5 * (4 - height), 5 * (4 - height) + 5):
            coupled_rows[r] = coupled(r)
    coupled_rows[15] = coupled(15)
    take(2)
    near_rows = [near(i) for i in range(2)]
    state = level(state, 1)
    near_rows += [near(i) for i in range(2, 8)]
    ends = [dot_t(state[i].astype(BF), basis_held[i]) for i in range(LEAVES)]
    take(3)
    near_rows += [near(i) for i in range(8, LEAVES)]
    for i in range(0, LEAVES, 2):
        span = slice(K * i, K * i + 128)
        pair = beside(ends[i], ends[i + 1])
        partial[:, span] = pair[:NV] + beside(near_rows[i], near_rows[i + 1])
        onward[:, span] = pair[NV:].astype(BF)


def top_kernel(roots, transfer, ids, partial, onward, shares, fifth, sixth, potential, nodes, held_ids, sems):
    device = lax.axis_index("leaf") * 2 + lax.axis_index("sub")
    id_copy = pltpu.make_async_copy(ids, held_ids, sems.at[0])
    id_copy.start()
    low4 = lax.broadcasted_iota(jnp.int32, (4, 128), 1) < K

    def pair(m):
        a, b = roots[2 * m].astype(F32), roots[2 * m + 1].astype(F32)
        upper = jnp.where(low4, a, pltpu.roll(b, K, 1))
        lower = jnp.where(low4, pltpu.roll(a, K, 1), b)
        return stacked(upper, lower)

    side = lax.broadcasted_iota(jnp.int32, (128, 2 * NV), 1) // NV
    blank, none = jnp.zeros((NV, 128), F32), jnp.zeros((128, 2 * NV), BF)
    made = []
    for m in range(32):
        rows = stacked(beside(pair(m), blank), beside(blank, pair(m + 32))).astype(BF)
        made.append(dot_t(beside(transfer[m], transfer[m + 32]), rows).astype(BF))
    for t, first in enumerate(FIRSTS):
        half = 32 >> t
        if 0 < t < 4:
            below, made = made, []
            for m in range(half):
                both = stacked(below[2 * m], below[2 * m + 1])
                both = stacked(jnp.where(side == 0, both, none), jnp.where(side == 1, both, none))
                made.append(dot(beside(transfer[first + m], transfer[first + half + m]), both).astype(BF))
        elif t >= 4:
            maps, span = (fifth, 4) if t == 4 else (sixth, 8)
            below, made = third, []
            for m in range(half):
                both = stacked(*below[span * m : span * m + span])
                ends = dot(maps[m], both), dot(maps[half + m], both)
                made.append(jnp.where(side[:K] == 0, *ends).astype(BF))
        if t == 2:
            third = made
        for m, node in enumerate(made):
            nodes[first + m] = node
    id_copy.wait()
    sources = []
    for t, first in enumerate(FIRSTS, 1):
        row, half = first + jnp.right_shift(device, t), 64 >> t
        for end in range(2):
            node = held_ids[end, row]
            upper_half = (node >= half).astype(jnp.int32)
            found = nodes[first + jnp.bitwise_and(node, half - 1)]
            sources.append(jnp.where(side[:K] == upper_half, found, none[:K]))
    incoming = dot(shares[...], stacked(*sources)).T
    incoming = (incoming[:NV] + incoming[NV:]).astype(BF)
    potential[...] = partial[...] + dot(incoming, onward[...])


def spec(space):
    return pl.BlockSpec(memory_space=space)


VMEM, SMEM, ANY = pltpu.VMEM, pltpu.SMEM, pl.ANY


def exchanged(core, pairs):
    return [(2 * a + core, 2 * b + core) for c, d in pairs for a, b in ((c, d), (d, c))]


INNER = exchanged(0, [(c, c + 1) for c in range(0, 64, 2)]) + exchanged(
    1, [(c, c + 2) for c in range(64) if c % 4 < 2]
)
OUTER = (
    exchanged(0, [(c, c + 1) for c in range(1, 63, 2)])
    + exchanged(1, [(c, c + 2) for c in range(62) if c % 4 >= 2])
    + [(0, 1), (1, 3), (3, 0), (126, 127), (127, 125), (125, 126)]
)


def local(
    density, basis, near_ids, near_count, near_blocks, local_transfer, local_coupling, local_coupling_ids,
    top_transfer, top_coupling, top_coupling_ids,
):
    shape = jax.ShapeDtypeStruct
    pack, roots = pl.pallas_call(
        upward_kernel,
        out_shape=(shape((PAIRS, NV, 128), BF), shape((128, 4, 128), BF)),
        in_specs=[spec(VMEM)] * 3,
        out_specs=(spec(VMEM),) * 2,
        cost_estimate=pl.CostEstimate(flops=20_000_000_000, bytes_accessed=1_000_000, transcendentals=0),
        compiler_params=pltpu.CompilerParams(vmem_limit_bytes=56 << 20),
        name="upward",
    )(density, basis, local_transfer)
    every = ("leaf", "sub")
    own = jnp.concatenate([pack, lax.ppermute(pack, "sub", [(0, 1), (1, 0)])])
    inner_mine = lax.ppermute(own, every, INNER)
    outer_mine = lax.ppermute(own, every, OUTER)
    all_roots = lax.all_to_all(roots, every, 0, 0, tiled=True)
    inner_other = lax.ppermute(inner_mine, "sub", [(0, 1), (1, 0)])
    outer_other = lax.ppermute(outer_mine, "sub", [(0, 1), (1, 0)])
    partial, onward, shares, fifth, sixth = pl.pallas_call(
        window_kernel,
        out_shape=(
            shape((NV, 1024), F32),
            shape((K, 1024), BF),
            shape((K, 768), BF),
            shape((4, K, 256), BF),
            shape((2, K, 512), BF),
        ),
        in_specs=[spec(ANY)] * 14,
        out_specs=(spec(VMEM),) * 5,
        scratch_shapes=[
            pltpu.VMEM((ZERO + 2, NV, 128), F32),
            pltpu.VMEM((5, 2 * PAIRS, NV, 128), BF),
            pltpu.VMEM((LEAVES, NEAR), jnp.int32),
            pltpu.VMEM((1, LEAVES), jnp.int32),
            pltpu.VMEM((COUP, 2 * LEAVES - 1), jnp.int32),
            pltpu.VMEM((LEAVES, NEAR), jnp.int32),
            pltpu.VMEM((COUP, 2 * LEAVES - 1), jnp.int32),
            pltpu.SMEM((LEAVES, NEAR), jnp.int32),
            pltpu.SMEM((COUP, 2 * LEAVES - 1), jnp.int32),
            pltpu.VMEM((LEAVES, 64, NEAR * 64), BF),
            pltpu.VMEM((2 * LEAVES - 1, K, COUP * K), BF),
            pltpu.VMEM((LEAVES - 1, K, 128), BF),
            pltpu.VMEM((LEAVES, 64, K), BF),
            pltpu.VMEM((6, K, 128), BF),
            pltpu.VMEM((6, K, 128), BF),
            pltpu.VMEM((14, K, 128), BF),
            pltpu.SemaphoreType.DMA((3,)),
            pltpu.SemaphoreType.DMA((2,)),
            pltpu.SemaphoreType.DMA((5,)),
            pltpu.SemaphoreType.DMA((4,)),
            pltpu.SemaphoreType.DMA((3,)),
            pltpu.SemaphoreType.DMA((2,)),
            pltpu.SemaphoreType.DMA((6,)),
            pltpu.SemaphoreType.DMA((6,)),
            pltpu.SemaphoreType.DMA((1,)),
        ],
        compiler_params=pltpu.CompilerParams(vmem_limit_bytes=52 << 20),
        cost_estimate=pl.CostEstimate(flops=120_000_000, bytes_accessed=8_000_000, transcendentals=0),
        name="window",
    )(
        own, inner_mine, inner_other, outer_mine, outer_other, near_ids, near_count.reshape(1, LEAVES),
        local_coupling_ids.T, near_blocks, local_coupling, local_transfer, basis, top_transfer, top_coupling,
    )
    return pl.pallas_call(
        top_kernel,
        out_shape=shape((NV, 1024), F32),
        in_specs=[spec(VMEM)] * 2 + [spec(ANY)] + [spec(VMEM)] * 5,
        out_specs=spec(VMEM),
        scratch_shapes=[
            pltpu.VMEM((TOP, K, 2 * NV), BF),
            pltpu.SMEM((2, TOP), jnp.int32),
            pltpu.SemaphoreType.DMA((1,)),
        ],
        compiler_params=pltpu.CompilerParams(vmem_limit_bytes=20 << 20),
        name="top",
    )(all_roots, top_transfer, top_coupling_ids.T, partial, onward, shares, fifth, sixth)


def solution(mesh):
    in_specs = (
        P(None, ("leaf", "sub")),
        P(("leaf", "sub"), None, None),
        P(("leaf", "sub"), None),
        P(("leaf", "sub")),
        P(("leaf", "sub"), None, None),
        P(("leaf", "sub"), None, None),
        P(("leaf", "sub"), None, None),
        P(("leaf", "sub"), None),
        P(),
        P(),
        P(),
    )
    out_specs = P(None, ("leaf", "sub"))
    return jax.shard_map(local, mesh=mesh, in_specs=in_specs, out_specs=out_specs, check_vma=False)
```
